512 devices in a mesh: dp: 32 (over z, core), owner: 16 (over x, y).
Axes of the slice: x: 4, y: 4, z: 16, core: 2. Of those that a mesh axis runs over, the one named last changes fastest.
Arguments:
- activations: bfloat16 [32768, 8192], P('dp', 'owner'), may hold values from -20 to 20
- key_cotangent: bfloat16 [32768, 1024], P('dp'), may hold values from -15 to 15
- block_owner: int32 [32], replicated, may hold values from 0 to 15, as said below
- left_root: bfloat16 [64, 512, 512], P('owner', 'dp'), may hold values from -1 to 5, as said below
- right_root: bfloat16 [64, 512, 512], P('owner'), may hold values from -1 to 3, as said below
Outputs:
- step_update: float32 [8192, 1024], P(('owner', 'dp'))
The draws below stay inside these ranges and needn't reach their ends.
Inputs may be any that keep to these rules, and one draw needn't show every extreme that they name: `block_owner`: each owner index is named by at most 4 blocks, and some owner by exactly 4. `left_root`: each slot's matrix is symmetric. `right_root`: each slot's matrix is symmetric.
All inputs are finite; a program needn't handle non-finite values.
Results may differ from the reference program's by a relative error of at most 0.0065.
Values may be sent and summed in bfloat16 or wider, within the bound.
No kernel may reach another device: no remote copies, remote signals or barrier semaphores. Data moves between devices by JAX's collectives and lax.ppermute only.
A program may use at most 128 MiB of HBM per device.

```python
import math
import jax
import jax.numpy as jnp
from jax import lax

BLOCK_EDGE = 512
KV = 1024
MAXB = 4
D = 8192
TOKENS = 32768
NBLK = 32
SLOT_TOTAL = 64
N_OWNER = 16


def draw_activations(key, part):
    key = jax.random.fold_in(key, 11)
    key_spread, key_noise = jax.random.split(key, 2)
    feature_ramp = 3.0 ** ((jnp.arange(D) % BLOCK_EDGE).astype(jnp.float32) / (BLOCK_EDGE - 1))
    spread = jnp.exp(jax.random.uniform(key_spread, (D,)) * math.log(4.0))
    column_scale = feature_ramp * spread / 3.0
    values = column_scale * jnp.clip(jax.random.normal(key_noise, (TOKENS, D)), -5.0, 5.0)
    return values.astype(jnp.bfloat16)


def draw_key_cotangent(key, part):
    key = jax.random.fold_in(key, 23)
    key_spread, key_noise = jax.random.split(key, 2)
    column_scale = 0.3 * jnp.exp(jax.random.uniform(key_spread, (KV,)) * math.log(10.0))
    values = column_scale * jnp.clip(jax.random.normal(key_noise, (TOKENS, KV)), -5.0, 5.0)
    return (values / math.sqrt(TOKENS)).astype(jnp.bfloat16)


def draw_block_owner(key, part):
    key = jax.random.fold_in(key, 37)
    key_blocks, key_owners = jax.random.split(key, 2)
    block_perm = jax.random.permutation(key_blocks, NBLK)
    owner_perm = jax.random.permutation(key_owners, N_OWNER)
    quarter = N_OWNER // 4
    place = jnp.arange(NBLK)
    rank = jnp.where(place < N_OWNER, place // 4, jnp.where(place < N_OWNER + 2 * quarter, quarter + (place - N_OWNER) // 2, 2 * quarter + (place - N_OWNER - 2 * quarter)))
    owner_by_place = owner_perm[rank]
    inverse = jnp.argsort(block_perm, stable=True)
    return owner_by_place[inverse].astype(jnp.int32)


def symmetric_root(key, lower_bound, upper_bound):
    key_offdiagonal, key_diagonal = jax.random.split(key, 2)
    unscaled_offdiagonal = jnp.clip(jax.random.normal(key_offdiagonal, (SLOT_TOTAL, BLOCK_EDGE, BLOCK_EDGE)), -5.0, 5.0)
    unscaled_offdiagonal = unscaled_offdiagonal / math.sqrt(BLOCK_EDGE)
    sym_off = (unscaled_offdiagonal + jnp.swapaxes(unscaled_offdiagonal, 1, 2)) / math.sqrt(2.0)
    diagonal_part = lower_bound * jnp.exp(jax.random.uniform(key_diagonal, (SLOT_TOTAL, BLOCK_EDGE)) * math.log(upper_bound / lower_bound))
    identity = (jnp.arange(BLOCK_EDGE)[:, None] == jnp.arange(BLOCK_EDGE)[None, :]).astype(jnp.float32)
    return sym_off + identity[None, :, :] * diagonal_part[:, :, None]


def draw_left_root(key, part):
    key = jax.random.fold_in(key, 41)
    return symmetric_root(key, 1.0, 4.0).astype(jnp.bfloat16)


def draw_right_root(key, part):
    key = jax.random.fold_in(key, 53)
    return symmetric_root(key, 0.5, 2.0).astype(jnp.bfloat16)


def setup_inputs(seed: int = 0) -> dict:
    arg_keys = jax.random.split(jax.random.key(seed), 6)
    return {
        "activations": draw_activations(jax.random.fold_in(arg_keys[5], 71), 0),
        "key_cotangent": draw_key_cotangent(jax.random.fold_in(arg_keys[5], 71), 0),
        "block_owner": draw_block_owner(jax.random.fold_in(arg_keys[5], 71), 0),
        "left_root": draw_left_root(jax.random.fold_in(arg_keys[5], 71), 0),
        "right_root": draw_right_root(jax.random.fold_in(arg_keys[5], 71), 0),
    }


def reference(activations, key_cotangent, block_owner, left_root, right_root):
    col_blocks = KV // BLOCK_EDGE
    gradient = lax.dot_general(activations, key_cotangent, (((0,), (0,)), ((), ())), preferred_element_type=jnp.float32)
    blocks = gradient.reshape(N_OWNER, BLOCK_EDGE, col_blocks, BLOCK_EDGE).transpose(0, 2, 1, 3).reshape(NBLK, BLOCK_EDGE, BLOCK_EDGE)
    block_ids = jnp.arange(NBLK, dtype=jnp.int32)
    same_owner = block_owner[:, None] == block_owner[None, :]
    slot_of = lax.optimization_barrier(jnp.sum((same_owner & (block_ids[None, :] < block_ids[:, None])).astype(jnp.int32), axis=1))
    slot_ids = (block_owner * MAXB + slot_of).astype(jnp.int32)
    lefts = left_root[slot_ids].astype(jnp.float32)
    rights = right_root[slot_ids].astype(jnp.float32)
    grads_low = blocks.astype(jnp.bfloat16).astype(jnp.float32)
    mixed = jnp.einsum('bij,bjk->bik', grads_low, rights, precision=lax.Precision.HIGHEST).astype(jnp.bfloat16)
    precond = jnp.einsum('bij,bjk->bik', lefts, mixed.astype(jnp.float32), precision=lax.Precision.HIGHEST)
    grad_sq = lax.optimization_barrier(jnp.sum(blocks * blocks, axis=(1, 2)))
    pre_sq = lax.optimization_barrier(jnp.sum(precond * precond, axis=(1, 2)))
    update = precond * jnp.sqrt(grad_sq / (pre_sq + 1e-06))[:, None, None]
    return update.reshape(N_OWNER, col_blocks, BLOCK_EDGE, BLOCK_EDGE).transpose(0, 2, 1, 3).reshape(D, KV)
```

```python
import jax
import jax.numpy as jnp
from jax import lax
from jax.experimental import pallas as pl
from jax.experimental.pallas import tpu as pltpu
from jax.sharding import Mesh
from jax.sharding import PartitionSpec as P

BF16 = jnp.bfloat16
F32 = jnp.float32
ROWS_FIRST = (((0,), (0,)), ((), ()))
ANY = pl.BlockSpec(memory_space=pl.ANY)
CORE, ZH, ZL, HOLDER, SLOTS = 0, 1, 2, 3, 4


def call(kernel, place, args, grid, in_specs, out_specs, out_shape, scratch=(), vmem=24):
    return pl.pallas_call(
        kernel,
        grid_spec=pltpu.PrefetchScalarGridSpec(
            num_scalar_prefetch=1, grid=grid, in_specs=in_specs, out_specs=out_specs, scratch_shapes=scratch
        ),
        out_shape=out_shape,
        compiler_params=pltpu.CompilerParams(vmem_limit_bytes=vmem * 1024 * 1024),
    )(place, *args)


def whole(*shape):
    return pl.BlockSpec(shape, lambda i, place: (0,) * len(shape))


def shape_of(shape, dtype):
    return jax.ShapeDtypeStruct(shape, dtype)


def theirs_kernel(place, acts, cots, out, acc):
    step = pl.program_id(0)
    part = lax.dot_general(acts[...], cots[...], ROWS_FIRST, preferred_element_type=F32)

    @pl.when(step == 0)
    def _():
        acc[...] = part

    @pl.when(step > 0)
    def _():
        acc[...] += part

    @pl.when(step == pl.num_programs(0) - 1)
    def _():
        out[...] = acc[...].astype(BF16)


def mine_kernel(place, acts, cots, swapped, own, up, down, across, acc):
    step = pl.program_id(0)
    part = lax.dot_general(acts[...], cots[...], ROWS_FIRST, preferred_element_type=F32)

    @pl.when(step == 0)
    def _():
        acc[...] = part + swapped[...].astype(F32)

    @pl.when(step > 0)
    def _():
        acc[...] += part

    @pl.when(step == pl.num_programs(0) - 1)
    def _():
        for ref, offset in ((own, 0), (up, 1), (down, 3), (across, 2)):
            rows = pl.ds(pl.multiple_of(lax.rem(place[ZL] + offset, 4) * 128, 128), 128)
            ref[...] = acc[rows, :].astype(ref.dtype)


def near_kernel(place, own, a, b, c, keep, up, down, across, acc):
    acc[...] = own[...] + a[...].astype(F32) + b[...].astype(F32) + c[...].astype(F32)
    for ref, offset in ((keep, 0), (up, 1), (down, 3), (across, 2)):
        rows = pl.ds(pl.multiple_of(lax.rem(place[ZH] + offset, 4) * 32, 32), 32)
        ref[...] = acc[rows, :].astype(ref.dtype)


def far_kernel(place, own, a, b, c, left, out):
    out[:, :512] = (own[...] + a[...].astype(F32) + b[...].astype(F32) + c[...].astype(F32)).astype(BF16)
    for j in range(3):
        lanes = pl.ds(pl.multiple_of(lax.rem(place[ZH] + j, 4) * 128, 128), 128)
        for half in range(2):
            out[16 * half : 16 * (half + 1), 512 + 128 * j : 640 + 128 * j] = left[half, 0, :, lanes]


def send_kernel(place, left, right, out, sems):
    copies = []
    for i in range(32):
        slot = place[SLOTS + i]
        copies.append(pltpu.make_async_copy(right.at[slot], out.at[i, pl.ds(0, 64)], sems.at[2 * i]))
        copies.append(pltpu.make_async_copy(left.at[slot], out.at[i, pl.ds(64, 16)], sems.at[2 * i + 1]))
    for copy in copies:
        copy.start()
    for copy in copies:
        copy.wait()


def middle_kernel(place, gathered, right, out):
    grad = gathered[:, :512]
    rows = right[:, 0].reshape(128, 512)
    mixed = lax.dot_general(grad, rows, (((1,), (1,)), ((), ())), preferred_element_type=F32).astype(BF16)
    pieces = [
        jnp.concatenate([mixed[32 * (4 * h + a) : 32 * (4 * h + a + 1)] for h in range(4)], axis=0) for a in range(4)
    ]
    pre_sq = jnp.zeros((), F32)
    for a in range(4):
        acc = jnp.zeros((128, 128), F32)
        for j in range(3):
            left = gathered[128 * a : 128 * (a + 1), 512 + 128 * j : 640 + 128 * j]
            acc += jnp.dot(left, pieces[(a + j) % 4], preferred_element_type=F32)
        b = (a + 3) % 4
        left = gathered[128 * b : 128 * (b + 1), 640:768]
        acc += lax.dot_general(left, pieces[b], ROWS_FIRST, preferred_element_type=F32)
        pre_sq += jnp.sum(acc * acc)

        @pl.when(place[ZH] == a)
        def _():
            out[:, :16, :] = acc.reshape(8, 16, 128)

    wide = grad.astype(F32)
    out[:, 16:20, :] = jnp.full((8, 4, 128), pre_sq, F32)
    out[:, 20:24, :] = jnp.full((8, 4, 128), jnp.sum(wide * wide), F32)


def shards(activations, key_cotangent, block_owner, left_root, right_root):
    core = lax.axis_index("core")
    owner = lax.axis_index("owner")
    zh = lax.axis_index("zh")
    zl = lax.axis_index("zl")

    block_ids = jnp.arange(32, dtype=jnp.int32)
    same_owner = block_owner[:, None] == block_owner[None, :]
    slot_of = jnp.sum((same_owner & (block_ids[None, :] < block_ids[:, None])).astype(jnp.int32), axis=1)
    send_slot = jnp.where(block_owner == owner, slot_of, 0).reshape(16, 2).T.reshape(32)
    holder = lax.dynamic_index_in_dim(block_owner, 2 * owner + core, 0, keepdims=False)
    place = jnp.concatenate([jnp.stack([core, zh, zl, holder]).astype(jnp.int32), send_slot])

    steps = 4
    chunk = 1024 // steps
    acts_spec = pl.BlockSpec((chunk, 512), lambda i, place: (i, 0))
    theirs = call(
        theirs_kernel, place, (activations, key_cotangent), (steps,),
        [acts_spec, pl.BlockSpec((chunk, 512), lambda i, place: (i, 1 - place[CORE]))],
        whole(512, 512), shape_of((512, 512), BF16), [pltpu.VMEM((512, 512), F32)],
    )
    swapped = lax.ppermute(theirs, "core", [(0, 1), (1, 0)])

    _, place_late = lax.optimization_barrier((theirs, place))
    sends = call(
        send_kernel, place_late, (left_root, right_root), (1,),
        [whole(4, 16, 512), pl.BlockSpec((4, 64, 512), lambda i, place: (0, 2 * place[ZL] + place[CORE], 0))],
        ANY, shape_of((32, 80, 512), BF16), [pltpu.SemaphoreType.DMA((64,))],
    )
    factors = lax.all_to_all(sends, ("core", "owner"), 0, 0, tiled=True).reshape(2, 16, 80, 512)

    piece = shape_of((128, 512), BF16)
    own, up, down, across = call(
        mine_kernel, place, (activations, key_cotangent, swapped), (steps,),
        [acts_spec, pl.BlockSpec((chunk, 512), lambda i, place: (i, place[CORE])), whole(512, 512)],
        [whole(128, 512)] * 4, [shape_of((128, 512), F32)] + [piece] * 3, [pltpu.VMEM((512, 512), F32)],
    )

    def shift(x, by):
        return lax.ppermute(x, ("zh", "zl"), [(i, (i + by) % 16) for i in range(16)])

    a, b, c = shift(up, 1), shift(down, -1), shift(across, 2)
    band = shape_of((32, 512), BF16)
    own, up, down, across = call(
        near_kernel, place, (own, a, b, c), (1,), [whole(128, 512)] * 4, [whole(32, 512)] * 4,
        [shape_of((32, 512), F32)] + [band] * 3, [pltpu.VMEM((128, 512), F32)],
    )
    a, b, c = shift(up, 4), shift(down, -4), shift(across, 8)
    left_spec = pl.BlockSpec((2, 1, 16, 512), lambda i, place: (0, place[HOLDER], 4, 0))
    part = call(
        far_kernel, place, (own, a, b, c, factors), (1,), [whole(32, 512)] * 4 + [left_spec],
        whole(32, 896), shape_of((32, 896), BF16),
    )
    gathered = lax.all_gather(part, ("zh", "zl"), axis=0, tiled=True)

    right_spec = pl.BlockSpec((2, 1, 64, 512), lambda i, place: (0, place[HOLDER], 0, 0))
    results = call(
        middle_kernel, place, (gathered, factors), (1,), [whole(512, 896), right_spec],
        whole(8, 24, 128), shape_of((8, 24, 128), F32),
    )
    got = lax.all_to_all(results, ("zl", "core"), 0, 0, tiled=True).reshape(4, 2, 24, 128)
    pre_sq = jnp.sum(got[:, :, 16, 0], axis=0)
    grad_sq = got[0, :, 20, 0]
    scale = jnp.sqrt(grad_sq / (pre_sq + 1e-06))
    update = got[:, :, :16, :] * scale[None, :, None, None]
    return update.transpose(2, 1, 0, 3).reshape(16, 1024)


def solution(mesh):
    split = Mesh(mesh.devices.reshape(4, 4, 2, 16), ("zh", "zl", "core", "owner"))
    dp = ("zh", "zl", "core")
    in_specs = (
        P(dp, "owner"),
        P(dp, None),
        P(),
        P("owner", dp, None),
        P("owner", None, None),
    )
    out_specs = P(("owner",) + dp, None)
    return jax.shard_map(shards, mesh=split, in_specs=in_specs, out_specs=out_specs, check_vma=False)
```

```python
import jax
import jax.numpy as jnp
from jax import lax
from jax.experimental import pallas as pl
from jax.experimental.pallas import tpu as pltpu
from jax.sharding import Mesh
from jax.sharding import PartitionSpec as P

BF16 = jnp.bfloat16
F32 = jnp.float32
ROWS_FIRST = (((0,), (0,)), ((), ()))
ANY = pl.BlockSpec(memory_space=pl.ANY)


def axis(name):
    return lax.axis_index(name)


def column():
    return axis("core") ^ (axis("zl") & 1)


def block_id():
    return 2 * axis("owner") + column()


def call(kernel, args, grid, in_specs, out_specs, out_shape, scratch=(), prefetch=0, vmem=24, cost=None):
    return pl.pallas_call(
        kernel,
        grid_spec=pltpu.PrefetchScalarGridSpec(
            num_scalar_prefetch=prefetch, grid=grid, in_specs=in_specs, out_specs=out_specs, scratch_shapes=scratch
        ),
        out_shape=out_shape,
        compiler_params=pltpu.CompilerParams(vmem_limit_bytes=vmem * 1024 * 1024),
        cost_estimate=cost,
    )(*args)


WAIT = pl.CostEstimate(flops=60_000_000_000, bytes_accessed=0, transcendentals=0)


def whole(*shape):
    return pl.BlockSpec(shape, lambda i, *_: (0,) * len(shape))


def shape_of(shape, dtype):
    return jax.ShapeDtypeStruct(shape, dtype)


def slots_to_send(owners, slots):
    held = jnp.int32(0)
    for b in range(32):
        hit = owners[b] == axis("owner")
        slots[b] = jnp.where(hit, held, 0)
        held += hit.astype(jnp.int32)


def send_kernel(owners, left, right, left_out, right_out, slots):
    slots_to_send(owners, slots)
    flip = axis("zl") & 1
    for i in range(16):
        right_out[i] = right[slots[2 * i + column()]]
        for core in range(2):
            left_out[16 * core + i] = left[slots[2 * i + (core ^ flip)]]


def split_kernel(mine, swapped, across, up, down, own):
    for ref, offset in ((across, 2), (up, 1), (down, 3), (own, 0)):
        for h in range(4):
            rows = pl.ds(pl.multiple_of(128 * h + 32 * lax.rem(axis("zl") + offset, 4), 32), 32)
            ref[32 * h : 32 * (h + 1)] = (mine[rows, :] + swapped[rows, :].astype(F32)).astype(ref.dtype)


def near_kernel(own, a, b, c, across, up, down, keep, acc):
    acc[...] = own[...] + a[...].astype(F32) + b[...].astype(F32) + c[...].astype(F32)
    for ref, offset in ((across, 2), (up, 1), (down, 3), (keep, 0)):
        rows = pl.ds(pl.multiple_of(lax.rem(axis("zh") + offset, 4) * 32, 32), 32)
        ref[...] = acc[rows, :].astype(ref.dtype)


def far_kernel(owners, own, a, b, c, left, out):
    out[:, :512] = (own[...] + a[...].astype(F32) + b[...].astype(F32) + c[...].astype(F32)).astype(BF16)
    for j in range(3):
        lanes = pl.ds(pl.multiple_of(lax.rem(axis("zh") + j, 4) * 128, 128), 128)
        for half in range(2):
            out[16 * half : 16 * (half + 1), 512 + 128 * j : 640 + 128 * j] = left[half, 0, :, lanes]


def middle_kernel(owners, gathered, rights, out, right, sem):
    fetch = pltpu.make_async_copy(rights.at[owners[block_id()]], right, sem)
    fetch.start()
    grad = gathered[:, :512]
    wide = grad.astype(F32)
    grad_sq = jnp.sum(wide * wide)
    fetch.wait()
    mixed = jnp.dot(right[...], grad, preferred_element_type=F32).astype(BF16)
    pieces = [mixed[:, 128 * b : 128 * (b + 1)] for b in range(4)]
    total = jnp.zeros((128, 128), F32)
    for a in range(4):
        left = gathered[128 * a : 128 * (a + 1), 640:768]
        acc = lax.dot_general(pieces[(a + 1) % 4], left, (((1,), (1,)), ((), ())), preferred_element_type=F32)
        for j in range(3):
            b = (a - j) % 4
            left = gathered[128 * b : 128 * (b + 1), 512 + 128 * j : 640 + 128 * j]
            acc += jnp.dot(pieces[b], left, preferred_element_type=F32)
        total += acc * acc

        @pl.when(axis("zh") == a)
        def _():
            out[:, :16, :] = acc.T.reshape(8, 16, 128)

    out[:, 16:20, :] = jnp.full((8, 4, 128), jnp.sum(total), F32)
    out[:, 20:24, :] = jnp.full((8, 4, 128), grad_sq, F32)


def place_kernel(got, out):
    for block in range(2):
        parts = [2 * l + (block ^ (l & 1)) for l in range(4)]
        pre_sq = sum(got[i, 16:17, :] for i in parts)
        scale = jnp.sqrt(got[parts[0], 20:21, :] / (pre_sq + 1e-06))
        for l, i in enumerate(parts):
            out[:, 512 * block + 128 * l : 512 * block + 128 * (l + 1)] = got[i, :16, :] * scale


def shards(activations, key_cotangent, block_owner, left_root, right_root):
    def product(half):
        columns = lax.dynamic_slice_in_dim(key_cotangent, half * 512, 512, 1)
        return lax.dot_general(columns, activations, ROWS_FIRST, preferred_element_type=F32)

    theirs = product(1 - column()).astype(BF16)
    swapped = lax.ppermute(theirs, "core", [(0, 1), (1, 0)])
    mine = product(column())

    left_sends, right_sends = call(
        send_kernel, (block_owner, left_root, right_root), (1,),
        [whole(4, 16, 512), pl.BlockSpec((4, 128, 512), lambda i, owners: (0, axis("zl"), 0))],
        [whole(32, 16, 512), whole(16, 128, 512)],
        [shape_of((32, 16, 512), BF16), shape_of((16, 128, 512), BF16)],
        [pltpu.SMEM((32,), jnp.int32)], prefetch=1,
    )

    piece = shape_of((128, 512), BF16)
    across, up, down, own = call(
        split_kernel, (mine, swapped), (1,), [whole(512, 512)] * 2,
        [whole(128, 512)] * 4, [piece] * 3 + [shape_of((128, 512), F32)],
    )
    own, left_sends = lax.optimization_barrier((own, left_sends))

    def shift(x, by):
        moves = [(i, (i + 2 * by) % 32 ^ (by & 1)) for i in range(32)]
        return lax.ppermute(x, ("zh", "zl", "core"), moves)

    a, b, c = shift(across, 2), shift(up, 1), shift(down, -1)
    lefts = lax.all_to_all(left_sends, ("core", "owner"), 0, 0, tiled=True).reshape(2, 16, 16, 512)
    band = shape_of((32, 512), BF16)
    across, up, down, own = call(
        near_kernel, (own, a, b, c), (1,), [whole(128, 512)] * 4, [whole(32, 512)] * 4,
        [band] * 3 + [shape_of((32, 512), F32)], [pltpu.VMEM((128, 512), F32)], cost=WAIT,
    )
    own, right_sends = lax.optimization_barrier((own, right_sends))
    a, b, c = shift(across, 8), shift(up, 4), shift(down, -4)
    rights = lax.all_to_all(right_sends, "owner", 0, 0, tiled=True)
    part = call(
        far_kernel, (block_owner, own, a, b, c, lefts), (1,),
        [whole(32, 512)] * 4 + [pl.BlockSpec((2, 1, 16, 512), lambda i, owners: (0, owners[block_id()], 0, 0))],
        whole(32, 896), shape_of((32, 896), BF16), prefetch=1, cost=WAIT,
    )
    groups = [[2 * z + (z & 1 ^ c) for z in range(16)] for c in range(2)]
    gathered = lax.all_gather(part, ("zh", "zl", "core"), axis=0, tiled=True, axis_index_groups=groups)

    results = call(
        middle_kernel, (block_owner, gathered, rights), (1,),
        [whole(512, 896), ANY], whole(8, 24, 128), shape_of((8, 24, 128), F32),
        [pltpu.VMEM((128, 512), BF16), pltpu.SemaphoreType.DMA], prefetch=1,
    )
    got = lax.all_to_all(results, ("zl", "core"), 0, 0, tiled=True)
    return call(place_kernel, (got,), (1,), [whole(8, 24, 128)], whole(16, 1024), shape_of((16, 1024), F32))


def solution(mesh):
    split = Mesh(mesh.devices.reshape(4, 4, 2, 16), ("zh", "zl", "core", "owner"))
    dp = ("zh", "zl", "core")
    in_specs = (
        P(dp, "owner"),
        P(dp, None),
        P(),
        P("owner", dp, None),
        P("owner", None, None),
    )
    out_specs = P(("owner",) + dp, None)
    return jax.shard_map(shards, mesh=split, in_specs=in_specs, out_specs=out_specs, check_vma=False)
```

```python
import jax
import jax.numpy as jnp
from jax import lax
from jax.experimental import pallas as pl
from jax.experimental.pallas import tpu as pltpu
from jax.sharding import Mesh
from jax.sharding import PartitionSpec as P

BF16 = jnp.bfloat16
F32 = jnp.float32
ROWS_FIRST = (((0,), (0,)), ((), ()))
ANY = pl.BlockSpec(memory_space=pl.ANY)


def axis(name):
    return lax.axis_index(name)


def column():
    return axis("core") ^ (axis("zl") & 1)


def block_id():
    return 2 * axis("owner") + column()


def call(kernel, args, grid, in_specs, out_specs, out_shape, scratch=(), prefetch=0, vmem=24, cost=None):
    return pl.pallas_call(
        kernel,
        grid_spec=pltpu.PrefetchScalarGridSpec(
            num_scalar_prefetch=prefetch, grid=grid, in_specs=in_specs, out_specs=out_specs, scratch_shapes=scratch
        ),
        out_shape=out_shape,
        compiler_params=pltpu.CompilerParams(vmem_limit_bytes=vmem * 1024 * 1024),
        cost_estimate=cost,
    )(*args)


WAIT = pl.CostEstimate(flops=60_000_000_000, bytes_accessed=0, transcendentals=0)


def whole(*shape):
    return pl.BlockSpec(shape, lambda i, *_: (0,) * len(shape))


def shape_of(shape, dtype):
    return jax.ShapeDtypeStruct(shape, dtype)


def slots_to_send(owners, slots):
    held = jnp.int32(0)
    for b in range(32):
        hit = owners[b] == axis("owner")
        slots[b] = jnp.where(hit, held, 0)
        held += hit.astype(jnp.int32)


def send_kernel(owners, left, right, left_out, right_out, slots):
    slots_to_send(owners, slots)
    flip = axis("zl") & 1
    for i in range(16):
        right_out[i] = right[slots[2 * i + column()]]
        for core in range(2):
            left_out[16 * core + i] = left[slots[2 * i + (core ^ flip)]]


def theirs_kernel(acts, cots, out, some_acts, some_cots, sems):
    lanes = pl.ds(pl.multiple_of((1 - column()) * 512, 512), 512)
    copies = []
    for i in range(4):
        rows = pl.ds(256 * i, 256)
        copies.append(pltpu.make_async_copy(cots.at[rows, lanes], some_cots.at[rows], sems.at[0, i]))
        copies.append(pltpu.make_async_copy(acts.at[rows], some_acts.at[rows], sems.at[1, i]))
    for copy in copies:
        copy.start()
    acc = jnp.zeros((512, 512), F32)
    for i in range(4):
        copies[2 * i].wait()
        copies[2 * i + 1].wait()
        rows = pl.ds(256 * i, 256)
        acc += lax.dot_general(some_cots[rows, :], some_acts[rows, :], ROWS_FIRST, preferred_element_type=F32)
    out[...] = acc.astype(BF16)


def holder(owners):
    lane = lax.broadcasted_iota(jnp.int32, (1, 32), 1)
    return jnp.sum(jnp.where(lane == block_id(), owners[...], 0))


def odd_even_kernel(mine, swapped, send, keep):
    here = axis("zl") & 1
    for h in range(8):
        for ref, side in ((send, 1 - here), (keep, here)):
            rows = pl.ds(pl.multiple_of(64 * h + 32 * side, 32), 32)
            ref[32 * h : 32 * (h + 1)] = (mine[rows, :] + swapped[rows, :].astype(F32)).astype(ref.dtype)


def quarter_kernel(kept, got, send, keep):
    here = axis("zl") >> 1
    for h in range(4):
        for ref, side in ((send, 1 - here), (keep, here)):
            rows = pl.ds(pl.multiple_of(64 * h + 32 * side, 32), 32)
            ref[32 * h : 32 * (h + 1)] = (kept[rows, :] + got[rows, :].astype(F32)).astype(ref.dtype)


def near_kernel(own, got, across, up, down, keep, acc):
    acc[...] = own[...] + got[...].astype(F32)
    for ref, offset in ((across, 2), (up, 1), (down, 3), (keep, 0)):
        rows = pl.ds(pl.multiple_of(lax.rem(axis("zh") + offset, 4) * 32, 32), 32)
        ref[...] = acc[rows, :].astype(ref.dtype)


def far_kernel(owners, own, a, b, c, left, out):
    held = holder(owners)
    out[:, :512] = (own[...] + a[...].astype(F32) + b[...].astype(F32) + c[...].astype(F32)).astype(BF16)
    for j in range(3):
        lanes = pl.ds(pl.multiple_of(lax.rem(axis("zh") + j, 4) * 128, 128), 128)
        for half in range(2):
            out[16 * half : 16 * (half + 1), 512 + 128 * j : 640 + 128 * j] = left[half, held, :, lanes]


def middle_kernel(owners, gathered, rights, out, right, sem):
    fetch = pltpu.make_async_copy(rights.at[holder(owners)], right, sem)
    fetch.start()
    grad = gathered[:, :512]
    wide = grad.astype(F32)
    grad_sq = jnp.sum(wide * wide)
    fetch.wait()
    mixed = jnp.dot(right[...], grad, preferred_element_type=F32).astype(BF16)
    pieces = [mixed[:, 128 * b : 128 * (b + 1)] for b in range(4)]
    total = jnp.zeros((128, 128), F32)
    for a in range(4):
        left = gathered[128 * a : 128 * (a + 1), 640:768]
        acc = lax.dot_general(pieces[(a + 1) % 4], left, (((1,), (1,)), ((), ())), preferred_element_type=F32)
        for j in range(3):
            b = (a - j) % 4
            left = gathered[128 * b : 128 * (b + 1), 512 + 128 * j : 640 + 128 * j]
            acc += jnp.dot(pieces[b], left, preferred_element_type=F32)
        total += acc * acc

        @pl.when(axis("zh") == a)
        def _():
            out[:, :16, :] = acc.T.reshape(8, 16, 128)

    out[:, 16:20, :] = jnp.full((8, 4, 128), jnp.sum(total), F32)
    out[:, 20:24, :] = jnp.full((8, 4, 128), grad_sq, F32)


def place_kernel(got, out):
    for block in range(2):
        parts = [2 * l + (block ^ (l & 1)) for l in range(4)]
        pre_sq = sum(got[i, 16:17, :] for i in parts)
        scale = jnp.sqrt(got[parts[0], 20:21, :] / (pre_sq + 1e-06))
        for l, i in enumerate(parts):
            out[:, 512 * block + 128 * l : 512 * block + 128 * (l + 1)] = got[i, :16, :] * scale


def shards(activations, key_cotangent, block_owner, left_root, right_root):
    hbm = pl.BlockSpec(memory_space=pltpu.HBM)
    theirs = pl.pallas_call(
        theirs_kernel, in_specs=[hbm] * 2, out_specs=pl.BlockSpec(memory_space=pltpu.VMEM),
        out_shape=shape_of((512, 512), BF16),
        scratch_shapes=[pltpu.VMEM((1024, 512), BF16)] * 2 + [pltpu.SemaphoreType.DMA((2, 4))],
        compiler_params=pltpu.CompilerParams(vmem_limit_bytes=60 * 1024 * 1024),
    )(activations, key_cotangent)
    swapped = lax.ppermute(theirs, "core", [(0, 1), (1, 0)])
    columns = lax.dynamic_slice_in_dim(key_cotangent, column() * 512, 512, 1)
    mine = lax.dot_general(columns, activations, ROWS_FIRST, preferred_element_type=F32)

    def shift(x, step, turned=False):
        moves = []
        for z in range(16):
            for block in range(2):
                to = (z + (-step if turned and block else step)) % 16
                moves.append((2 * z + (block ^ (z & 1)), 2 * to + (block ^ (to & 1))))
        return lax.ppermute(x, ("zh", "zl", "core"), moves)

    send, own = call(
        odd_even_kernel, (mine, swapped), (1,), [whole(512, 512)] * 2,
        [whole(256, 512)] * 2, [shape_of((256, 512), BF16), shape_of((256, 512), F32)],
    )
    got = shift(send, 1, True)

    owner_row = block_owner.reshape(1, 32)
    own, block_owner = lax.optimization_barrier((own, block_owner))
    left_sends, right_sends = call(
        send_kernel, (block_owner, left_root, right_root), (1,),
        [whole(4, 16, 512), pl.BlockSpec((4, 128, 512), lambda i, owners: (0, axis("zl"), 0))],
        [whole(32, 16, 512), whole(16, 128, 512)],
        [shape_of((32, 16, 512), BF16), shape_of((16, 128, 512), BF16)],
        [pltpu.SMEM((32,), jnp.int32)], prefetch=1,
    )

    own, left_sends, right_sends = lax.optimization_barrier((own, left_sends, right_sends))
    send, own = call(
        quarter_kernel, (own, got), (1,), [whole(256, 512)] * 2,
        [whole(128, 512)] * 2, [shape_of((128, 512), BF16), shape_of((128, 512), F32)],
    )
    own, left_sends = lax.optimization_barrier((own, left_sends))
    lefts = lax.all_to_all(left_sends, ("core", "owner"), 0, 0, tiled=True).reshape(2, 16, 16, 512)
    got = shift(send, 2, True)
    band = shape_of((32, 512), BF16)
    across, up, down, own = call(
        near_kernel, (own, got), (1,), [whole(128, 512)] * 2, [whole(32, 512)] * 4,
        [band] * 3 + [shape_of((32, 512), F32)], [pltpu.VMEM((128, 512), F32)], cost=WAIT,
    )
    own, right_sends = lax.optimization_barrier((own, right_sends))
    a, b, c = shift(across, 8), shift(up, 4), shift(down, -4)
    rights = lax.all_to_all(right_sends, "owner", 0, 0, tiled=True)
    part = call(
        far_kernel, (owner_row, own, a, b, c, lefts), (1,),
        [whole(1, 32)] + [whole(32, 512)] * 4 + [whole(2, 16, 16, 512)],
        whole(32, 896), shape_of((32, 896), BF16), cost=WAIT,
    )
    groups = [[2 * z + (z & 1 ^ c) for z in range(16)] for c in range(2)]
    gathered = lax.all_gather(part, ("zh", "zl", "core"), axis=0, tiled=True, axis_index_groups=groups)

    results = call(
        middle_kernel, (owner_row, gathered, rights), (1,),
        [whole(1, 32), whole(512, 896), ANY], whole(8, 24, 128), shape_of((8, 24, 128), F32),
        [pltpu.VMEM((128, 512), BF16), pltpu.SemaphoreType.DMA],
    )
    got = lax.all_to_all(results, ("zl", "core"), 0, 0, tiled=True)
    return call(place_kernel, (got,), (1,), [whole(8, 24, 128)], whole(16, 1024), shape_of((16, 1024), F32))


def solution(mesh):
    split = Mesh(mesh.devices.reshape(4, 4, 2, 16), ("zh", "zl", "core", "owner"))
    dp = ("zh", "zl", "core")
    in_specs = (
        P(dp, "owner"),
        P(dp, None),
        P(),
        P("owner", dp, None),
        P("owner", None, None),
    )
    out_specs = P(("owner",) + dp, None)
    return jax.shard_map(shards, mesh=split, in_specs=in_specs, out_specs=out_specs, check_vma=False)
```

```python
import jax
import jax.numpy as jnp
from jax import lax
from jax.experimental import pallas as pl
from jax.experimental.pallas import tpu as pltpu
from jax.sharding import Mesh
from jax.sharding import PartitionSpec as P

BF16 = jnp.bfloat16
F32 = jnp.float32
ROWS_FIRST = (((0,), (0,)), ((), ()))
ANY = pl.BlockSpec(memory_space=pl.ANY)


def axis(name):
    return lax.axis_index(name)


def column():
    return axis("core") ^ (axis("zl") & 1)


def block_id():
    return 2 * axis("owner") + column()


def call(kernel, args, grid, in_specs, out_specs, out_shape, scratch=(), prefetch=0, vmem=24, cost=None):
    return pl.pallas_call(
        kernel,
        grid_spec=pltpu.PrefetchScalarGridSpec(
            num_scalar_prefetch=prefetch, grid=grid, in_specs=in_specs, out_specs=out_specs, scratch_shapes=scratch
        ),
        out_shape=out_shape,
        compiler_params=pltpu.CompilerParams(vmem_limit_bytes=vmem * 1024 * 1024),
        cost_estimate=cost,
    )(*args)


WAIT = pl.CostEstimate(flops=60_000_000_000, bytes_accessed=0, transcendentals=0)


def whole(*shape):
    return pl.BlockSpec(shape, lambda i, *_: (0,) * len(shape))


def shape_of(shape, dtype):
    return jax.ShapeDtypeStruct(shape, dtype)


def slots_to_send(owners, slots):
    held = jnp.int32(0)
    for b in range(32):
        hit = owners[b] == axis("owner")
        slots[b] = jnp.where(hit, held, 0)
        held += hit.astype(jnp.int32)


def send_left_kernel(owners, left, out, slots):
    slots_to_send(owners, slots)
    flip = axis("zl") & 1
    for i in range(32):
        out[i] = left[slots[2 * (i % 16) + (i // 16 ^ flip)]]


def send_right_kernel(owners, right, out, slots):
    slots_to_send(owners, slots)
    for i in range(16):
        out[i] = right[slots[2 * i + column()]]


def theirs_kernel(acts, cots, out, some_acts, some_cots, sems):
    lanes = pl.ds(pl.multiple_of((1 - column()) * 512, 512), 512)
    copies = []
    for i in range(4):
        rows = pl.ds(256 * i, 256)
        copies.append(pltpu.make_async_copy(cots.at[rows, lanes], some_cots.at[rows], sems.at[0, i]))
        copies.append(pltpu.make_async_copy(acts.at[rows], some_acts.at[rows], sems.at[1, i]))
    for copy in copies:
        copy.start()
    acc = jnp.zeros((512, 512), F32)
    for i in range(4):
        copies[2 * i].wait()
        copies[2 * i + 1].wait()
        rows = pl.ds(256 * i, 256)
        acc += lax.dot_general(some_cots[rows, :], some_acts[rows, :], ROWS_FIRST, preferred_element_type=F32)
    out[...] = acc.astype(BF16)


def holder(owners):
    lane = lax.broadcasted_iota(jnp.int32, (1, 32), 1)
    return jnp.sum(jnp.where(lane == block_id(), owners[...], 0))


def half_kernel(mine, swapped, send, keep):
    for j in range(4):
        ref = send if j > 1 else keep
        first = 32 * lax.rem(axis("zl") + j * (1 + 2 * column()), 4)
        for h in range(4):
            rows = pl.ds(pl.multiple_of(128 * h + first, 32), 32)
            here = slice(128 * (j % 2) + 32 * h, 128 * (j % 2) + 32 * (h + 1))
            ref[here] = (mine[rows, :] + swapped[rows, :].astype(F32)).astype(ref.dtype)


def quarter_kernel(kept, got, send, keep):
    keep[...] = kept[:128] + got[:128].astype(F32)
    send[...] = (kept[128:] + got[128:].astype(F32)).astype(BF16)


def near_kernel(own, got, across, up, down, keep, acc):
    acc[...] = own[...] + got[...].astype(F32)
    for ref, offset in ((across, 2), (up, 1), (down, 3), (keep, 0)):
        rows = pl.ds(pl.multiple_of(lax.rem(axis("zh") + offset, 4) * 32, 32), 32)
        ref[...] = acc[rows, :].astype(ref.dtype)


def far_kernel(owners, own, a, b, c, left, out):
    held = holder(owners)
    out[:, :512] = (own[...] + a[...].astype(F32) + b[...].astype(F32) + c[...].astype(F32)).astype(BF16)
    for j in range(3):
        lanes = pl.ds(pl.multiple_of(lax.rem(axis("zh") + j, 4) * 128, 128), 128)
        for half in range(2):
            out[16 * half : 16 * (half + 1), 512 + 128 * j : 640 + 128 * j] = left[half, held, :, lanes]


def middle_kernel(owners, gathered, rights, out, right, sem):
    fetch = pltpu.make_async_copy(rights.at[holder(owners)], right, sem)
    fetch.start()
    grad = gathered[:, :512]
    wide = grad.astype(F32)
    grad_sq = jnp.sum(jnp.sum(wide * wide, axis=0, keepdims=True), axis=1, keepdims=True)
    fetch.wait()
    mixed = jnp.dot(right[...], grad, preferred_element_type=F32).astype(BF16)
    mixed = mixed.T
    pieces = [mixed[128 * b : 128 * (b + 1)] for b in range(4)]
    total = jnp.zeros((128, 128), F32)
    for a in range(4):
        left = gathered[128 * a : 128 * (a + 1), 512:896]
        turn = gathered[128 * ((a + 3) % 4) : 128 * ((a + 3) % 4 + 1), 640:768]
        three = jnp.concatenate([pieces[(a + j) % 4] for j in range(3)], axis=0)
        acc = jnp.dot(left, three, preferred_element_type=F32)
        acc += lax.dot_general(turn, pieces[(a + 3) % 4], ROWS_FIRST, preferred_element_type=F32)
        total += acc * acc

        @pl.when(axis("zh") == a)
        def _():
            out[:, :16, :] = acc.astype(BF16).reshape(8, 16, 128)

    pre_sq = jnp.sum(jnp.sum(total, axis=0, keepdims=True), axis=1, keepdims=True)
    row = lax.broadcasted_iota(jnp.int32, (16, 128), 0)
    rest = jnp.where(row < 8, pre_sq, grad_sq)
    terms = jnp.zeros((16, 128), F32)
    for i in range(3):
        term = rest.astype(BF16).astype(F32)
        terms = jnp.where(row % 8 == i, term, terms)
        rest -= term
    out[:, 16:, :] = jnp.broadcast_to(terms.astype(BF16)[None], (8, 16, 128))


def place_kernel(got, out):
    def total(part, first):
        return sum(got[part, first + i : first + i + 1, :].astype(F32) for i in (2, 1, 0))

    for block in range(2):
        parts = [2 * l + (block ^ (l & 1)) for l in range(4)]
        pre_sq = sum(total(i, 16) for i in parts)
        scale = jnp.sqrt(total(parts[0], 24) / (pre_sq + 1e-06))
        for l, i in enumerate(parts):
            out[:, 512 * block + 128 * l : 512 * block + 128 * (l + 1)] = got[i, :16, :].astype(F32) * scale


def shards(activations, key_cotangent, block_owner, left_root, right_root):
    hbm = pl.BlockSpec(memory_space=pltpu.HBM)
    theirs = pl.pallas_call(
        theirs_kernel, in_specs=[hbm] * 2, out_specs=pl.BlockSpec(memory_space=pltpu.VMEM),
        out_shape=shape_of((512, 512), BF16),
        scratch_shapes=[pltpu.VMEM((1024, 512), BF16)] * 2 + [pltpu.SemaphoreType.DMA((2, 4))],
        compiler_params=pltpu.CompilerParams(vmem_limit_bytes=60 * 1024 * 1024),
    )(activations, key_cotangent)
    swapped = lax.ppermute(theirs, "core", [(0, 1), (1, 0)])
    columns = lax.dynamic_slice_in_dim(key_cotangent, column() * 512, 512, 1)
    mine = lax.dot_general(columns, activations, ROWS_FIRST, preferred_element_type=F32)

    def shift(x, step, turned=False):
        moves = []
        for z in range(16):
            for block in range(2):
                to = (z + (-step if turned and block else step)) % 16
                moves.append((2 * z + (block ^ (z & 1)), 2 * to + (block ^ (to & 1))))
        return lax.ppermute(x, ("zh", "zl", "core"), moves)

    send, own = call(
        half_kernel, (mine, swapped), (1,), [whole(512, 512)] * 2,
        [whole(256, 512)] * 2, [shape_of((256, 512), BF16), shape_of((256, 512), F32)],
    )
    got = shift(send, 2, True)

    owner_row = block_owner.reshape(1, 32)
    own, block_owner = lax.optimization_barrier((own, block_owner))
    left_sends = call(
        send_left_kernel, (block_owner, left_root), (1,), [whole(4, 16, 512)], whole(32, 16, 512),
        shape_of((32, 16, 512), BF16), [pltpu.SMEM((32,), jnp.int32)], prefetch=1,
    )
    lefts = lax.all_to_all(left_sends, ("core", "owner"), 0, 0, tiled=True).reshape(2, 16, 16, 512)
    own, left_sends = lax.optimization_barrier((own, left_sends))
    send, own = call(
        quarter_kernel, (own, got), (1,), [whole(256, 512)] * 2,
        [whole(128, 512)] * 2, [shape_of((128, 512), BF16), shape_of((128, 512), F32)], cost=WAIT,
    )
    got = shift(send, 1, True)
    own, block_owner = lax.optimization_barrier((own, block_owner))
    right_sends = call(
        send_right_kernel, (block_owner, right_root), (1,),
        [pl.BlockSpec((4, 128, 512), lambda i, owners: (0, axis("zl"), 0))],
        whole(16, 128, 512), shape_of((16, 128, 512), BF16), [pltpu.SMEM((32,), jnp.int32)], prefetch=1,
    )
    own, right_sends = lax.optimization_barrier((own, right_sends))
    band = shape_of((32, 512), BF16)
    across, up, down, own = call(
        near_kernel, (own, got), (1,), [whole(128, 512)] * 2, [whole(32, 512)] * 4,
        [band] * 3 + [shape_of((32, 512), F32)], [pltpu.VMEM((128, 512), F32)],
    )
    own, right_sends = lax.optimization_barrier((own, right_sends))
    a, b, c = shift(across, 8), shift(up, 4), shift(down, -4)
    rights = lax.all_to_all(right_sends, "owner", 0, 0, tiled=True)
    part = call(
        far_kernel, (owner_row, own, a, b, c, lefts), (1,),
        [whole(1, 32)] + [whole(32, 512)] * 4 + [whole(2, 16, 16, 512)],
        whole(32, 896), shape_of((32, 896), BF16), cost=WAIT,
    )
    groups = [[2 * z + (z & 1 ^ c) for z in range(16)] for c in range(2)]
    gathered = lax.all_gather(part, ("zh", "zl", "core"), axis=0, tiled=True, axis_index_groups=groups)

    results = call(
        middle_kernel, (owner_row, gathered, rights), (1,),
        [whole(1, 32), whole(512, 896), ANY], whole(8, 32, 128), shape_of((8, 32, 128), BF16),
        [pltpu.VMEM((128, 512), BF16), pltpu.SemaphoreType.DMA],
    )
    got = lax.all_to_all(results, ("zl", "core"), 0, 0, tiled=True)
    return call(place_kernel, (got,), (1,), [whole(8, 32, 128)], whole(16, 1024), shape_of((16, 1024), F32))


def solution(mesh):
    split = Mesh(mesh.devices.reshape(4, 4, 2, 16), ("zh", "zl", "core", "owner"))
    dp = ("zh", "zl", "core")
    in_specs = (
        P(dp, "owner"),
        P(dp, None),
        P(),
        P("owner", dp, None),
        P("owner", None, None),
    )
    out_specs = P(("owner",) + dp, None)
    return jax.shard_map(shards, mesh=split, in_specs=in_specs, out_specs=out_specs, check_vma=False)
```

```python
import jax
import jax.numpy as jnp
from jax import lax
from jax.experimental import pallas as pl
from jax.experimental.pallas import tpu as pltpu
from jax.sharding import Mesh
from jax.sharding import PartitionSpec as P

BF16 = jnp.bfloat16
F32 = jnp.float32
ROWS_FIRST = (((0,), (0,)), ((), ()))
ANY = pl.BlockSpec(memory_space=pl.ANY)


def axis(name):
    return lax.axis_index(name)


def column():
    return axis("core") ^ (axis("zl") & 1)


def block_id():
    return 2 * axis("owner") + column()


def call(kernel, args, grid, in_specs, out_specs, out_shape, scratch=(), prefetch=0, vmem=24, cost=None):
    return pl.pallas_call(
        kernel,
        grid_spec=pltpu.PrefetchScalarGridSpec(
            num_scalar_prefetch=prefetch, grid=grid, in_specs=in_specs, out_specs=out_specs, scratch_shapes=scratch
        ),
        out_shape=out_shape,
        compiler_params=pltpu.CompilerParams(vmem_limit_bytes=vmem * 1024 * 1024),
        cost_estimate=cost,
    )(*args)


WAIT = pl.CostEstimate(flops=60_000_000_000, bytes_accessed=0, transcendentals=0)


def whole(*shape):
    return pl.BlockSpec(shape, lambda i, *_: (0,) * len(shape))


def shape_of(shape, dtype):
    return jax.ShapeDtypeStruct(shape, dtype)


def slots_to_send(owners, slots):
    held = jnp.int32(0)
    for b in range(32):
        hit = owners[b] == axis("owner")
        slots[b] = jnp.where(hit, held, 0)
        held += hit.astype(jnp.int32)


def send_kernel(owners, left, right, left_out, right_out, slots):
    slots_to_send(owners, slots)
    flip = axis("zl") & 1
    for i in range(16):
        right_out[i] = right[slots[2 * i + column()]]
        for core in range(2):
            for j in range(3):
                lanes = pl.ds(pl.multiple_of(lax.rem(axis("zh") + j, 4) * 128, 128), 128)
                left_out[16 * core + i, :, 128 * j : 128 * (j + 1)] = left[slots[2 * i + (core ^ flip)], :, lanes]


def theirs_kernel(acts, cots, out, some_acts, some_cots, sems):
    lanes = pl.ds(pl.multiple_of((1 - column()) * 512, 512), 512)
    copies = []
    for i in range(4):
        rows = pl.ds(256 * i, 256)
        copies.append(pltpu.make_async_copy(cots.at[rows, lanes], some_cots.at[rows], sems.at[0, i]))
        copies.append(pltpu.make_async_copy(acts.at[rows], some_acts.at[rows], sems.at[1, i]))
    for copy in copies:
        copy.start()
    acc = jnp.zeros((512, 512), F32)
    for i in range(4):
        copies[2 * i].wait()
        copies[2 * i + 1].wait()
        rows = pl.ds(256 * i, 256)
        acc += lax.dot_general(some_cots[rows, :], some_acts[rows, :], ROWS_FIRST, preferred_element_type=F32)
    out[...] = acc.astype(BF16)


def holder(owners):
    lane = lax.broadcasted_iota(jnp.int32, (1, 32), 1)
    return jnp.sum(jnp.where(lane == block_id(), owners[...], 0))


def split_kernel(mine, swapped, across, up, down, own):
    for ref, offset in ((across, 2), (up, 1 + 2 * column()), (down, 3 - 2 * column()), (own, 0)):
        first = 32 * lax.rem(axis("zl") + offset, 4)
        for h in range(4):
            rows = pl.ds(pl.multiple_of(128 * h + first, 32), 32)
            ref[32 * h : 32 * (h + 1)] = (mine[rows, :] + swapped[rows, :].astype(F32)).astype(ref.dtype)


def near_kernel(own, a, b, c, send, keep, acc):
    acc[...] = own[...] + a[...].astype(F32) + b[...].astype(F32) + c[...].astype(F32)
    other = axis("zh") + 1 + 2 * column()
    for ref, first in ((send, other), (keep, axis("zh"))):
        for j in range(2):
            rows = pl.ds(pl.multiple_of(lax.rem(first + 2 * j, 4) * 32, 32), 32)
            ref[32 * j : 32 * (j + 1)] = acc[rows, :].astype(ref.dtype)


def pair_kernel(kept, got, send, keep):
    keep[...] = kept[:32] + got[:32].astype(F32)
    send[...] = (kept[32:] + got[32:].astype(F32)).astype(BF16)


def far_kernel(owners, own, got, left, out):
    held = holder(owners)
    out[:, :512] = (own[...] + got[...].astype(F32)).astype(BF16)
    for half in range(2):
        out[16 * half : 16 * (half + 1), 512:] = left[half, held]


def middle_kernel(owners, gathered, rights, out, right, sem):
    fetch = pltpu.make_async_copy(rights.at[holder(owners)], right, sem)
    fetch.start()
    grad = gathered[:, :512]
    wide = grad.astype(F32)
    grad_sq = jnp.sum(jnp.sum(wide * wide, axis=0, keepdims=True), axis=1, keepdims=True)
    fetch.wait()
    mixed = jnp.dot(right[...], grad, preferred_element_type=F32).astype(BF16)
    mixed = mixed.T
    pieces = [mixed[128 * b : 128 * (b + 1)] for b in range(4)]
    total = jnp.zeros((128, 128), F32)
    for a in range(4):
        left = gathered[128 * a : 128 * (a + 1), 512:896]
        turn = gathered[128 * ((a + 3) % 4) : 128 * ((a + 3) % 4 + 1), 640:768]
        three = jnp.concatenate([pieces[(a + j) % 4] for j in range(3)], axis=0)
        acc = jnp.dot(left, three, preferred_element_type=F32)
        acc += lax.dot_general(turn, pieces[(a + 3) % 4], ROWS_FIRST, preferred_element_type=F32)
        total += acc * acc

        @pl.when(axis("zh") == a)
        def _():
            out[:, :16, :] = acc.astype(BF16).reshape(8, 16, 128)

    pre_sq = jnp.sum(jnp.sum(total, axis=0, keepdims=True), axis=1, keepdims=True)
    row = lax.broadcasted_iota(jnp.int32, (16, 128), 0)
    rest = jnp.where(row < 8, pre_sq, grad_sq)
    terms = jnp.zeros((16, 128), F32)
    for i in range(3):
        term = rest.astype(BF16).astype(F32)
        terms = jnp.where(row % 8 == i, term, terms)
        rest -= term
    out[:, 16:, :] = jnp.broadcast_to(terms.astype(BF16)[None], (8, 16, 128))


def place_kernel(got, out):
    def total(part, first):
        return sum(got[part, first + i : first + i + 1, :].astype(F32) for i in (2, 1, 0))

    for block in range(2):
        parts = [2 * l + (block ^ (l & 1)) for l in range(4)]
        pre_sq = sum(total(i, 16) for i in parts)
        scale = jnp.sqrt(total(parts[0], 24) / (pre_sq + 1e-06))
        for l, i in enumerate(parts):
            out[:, 512 * block + 128 * l : 512 * block + 128 * (l + 1)] = got[i, :16, :].astype(F32) * scale


def shards(activations, key_cotangent, block_owner, left_root, right_root):
    hbm = pl.BlockSpec(memory_space=pltpu.HBM)
    theirs = pl.pallas_call(
        theirs_kernel, in_specs=[hbm] * 2, out_specs=pl.BlockSpec(memory_space=pltpu.VMEM),
        out_shape=shape_of((512, 512), BF16),
        scratch_shapes=[pltpu.VMEM((1024, 512), BF16)] * 2 + [pltpu.SemaphoreType.DMA((2, 4))],
        compiler_params=pltpu.CompilerParams(vmem_limit_bytes=60 * 1024 * 1024),
    )(activations, key_cotangent)
    swapped = lax.ppermute(theirs, "core", [(0, 1), (1, 0)])
    columns = lax.dynamic_slice_in_dim(key_cotangent, column() * 512, 512, 1)
    mine = lax.dot_general(columns, activations, ROWS_FIRST, preferred_element_type=F32)

    def shift(x, step):
        moves = []
        for z in range(16):
            for block in range(2):
                to = (z + (-step if block else step)) % 16
                moves.append((2 * z + (block ^ (z & 1)), 2 * to + (block ^ (to & 1))))
        return lax.ppermute(x, ("zh", "zl", "core"), moves)

    quarter = shape_of((128, 512), BF16)
    across, up, down, own = call(
        split_kernel, (mine, swapped), (1,), [whole(512, 512)] * 2,
        [whole(128, 512)] * 4, [quarter] * 3 + [shape_of((128, 512), F32)],
    )
    a, b, c = shift(across, 2), shift(up, 1), shift(down, -1)

    owner_row = block_owner.reshape(1, 32)
    own, block_owner = lax.optimization_barrier((own, block_owner))
    left_sends, right_sends = call(
        send_kernel, (block_owner, left_root, right_root), (1,),
        [whole(4, 16, 512), pl.BlockSpec((4, 128, 512), lambda i, owners: (0, axis("zl"), 0))],
        [whole(32, 16, 384), whole(16, 128, 512)],
        [shape_of((32, 16, 384), BF16), shape_of((16, 128, 512), BF16)],
        [pltpu.SMEM((32,), jnp.int32)], prefetch=1,
    )
    own, left_sends, right_sends = lax.optimization_barrier((own, left_sends, right_sends))
    send, own = call(
        near_kernel, (own, a, b, c), (1,), [whole(128, 512)] * 4, [whole(64, 512)] * 2,
        [shape_of((64, 512), BF16), shape_of((64, 512), F32)], [pltpu.VMEM((128, 512), F32)], cost=WAIT,
    )
    own, left_sends = lax.optimization_barrier((own, left_sends))
    lefts = lax.all_to_all(left_sends, ("core", "owner"), 0, 0, tiled=True).reshape(2, 16, 16, 384)
    got = shift(send, 4)
    send, own = call(
        pair_kernel, (own, got), (1,), [whole(64, 512)] * 2, [whole(32, 512)] * 2,
        [shape_of((32, 512), BF16), shape_of((32, 512), F32)], cost=WAIT,
    )
    own, right_sends = lax.optimization_barrier((own, right_sends))
    got = shift(send, 8)
    rights = lax.all_to_all(right_sends, "owner", 0, 0, tiled=True)
    part = call(
        far_kernel, (owner_row, own, got, lefts), (1,),
        [whole(1, 32)] + [whole(32, 512)] * 2 + [whole(2, 16, 16, 384)],
        whole(32, 896), shape_of((32, 896), BF16), cost=WAIT,
    )
    groups = [[2 * z + (z & 1 ^ c) for z in range(16)] for c in range(2)]
    gathered = lax.all_gather(part, ("zh", "zl", "core"), axis=0, tiled=True, axis_index_groups=groups)

    results = call(
        middle_kernel, (owner_row, gathered, rights), (1,),
        [whole(1, 32), whole(512, 896), ANY], whole(8, 32, 128), shape_of((8, 32, 128), BF16),
        [pltpu.VMEM((128, 512), BF16), pltpu.SemaphoreType.DMA],
    )
    got = lax.all_to_all(results, ("zl", "core"), 0, 0, tiled=True)
    return call(place_kernel, (got,), (1,), [whole(8, 32, 128)], whole(16, 1024), shape_of((16, 1024), F32))


def solution(mesh):
    split = Mesh(mesh.devices.reshape(4, 4, 2, 16), ("zh", "zl", "core", "owner"))
    dp = ("zh", "zl", "core")
    in_specs = (
        P(dp, "owner"),
        P(dp, None),
        P(),
        P("owner", dp, None),
        P("owner", None, None),
    )
    out_specs = P(("owner",) + dp, None)
    return jax.shard_map(shards, mesh=split, in_specs=in_specs, out_specs=out_specs, check_vma=False)
```

```python
import jax
import jax.numpy as jnp
from jax import lax
from jax.experimental import pallas as pl
from jax.experimental.pallas import tpu as pltpu
from jax.sharding import Mesh
from jax.sharding import PartitionSpec as P

BF16 = jnp.bfloat16
F32 = jnp.float32
ROWS_FIRST = (((0,), (0,)), ((), ()))
ANY = pl.BlockSpec(memory_space=pl.ANY)


def axis(name):
    return lax.axis_index(name)


def column():
    return axis("core") ^ (axis("zl") & 1)


def block_id():
    return 2 * axis("owner") + column()


def call(kernel, args, grid, in_specs, out_specs, out_shape, scratch=(), prefetch=0, vmem=24, cost=None):
    return pl.pallas_call(
        kernel,
        grid_spec=pltpu.PrefetchScalarGridSpec(
            num_scalar_prefetch=prefetch, grid=grid, in_specs=in_specs, out_specs=out_specs, scratch_shapes=scratch
        ),
        out_shape=out_shape,
        compiler_params=pltpu.CompilerParams(vmem_limit_bytes=vmem * 1024 * 1024),
        cost_estimate=cost,
    )(*args)


WAIT = pl.CostEstimate(flops=60_000_000_000, bytes_accessed=0, transcendentals=0)


def whole(*shape):
    return pl.BlockSpec(shape, lambda i, *_: (0,) * len(shape))


def shape_of(shape, dtype):
    return jax.ShapeDtypeStruct(shape, dtype)


def slots_to_send(owners, slots):
    held = jnp.int32(0)
    for b in range(32):
        hit = owners[b] == axis("owner")
        slots[b] = jnp.where(hit, held, 0)
        held += hit.astype(jnp.int32)


def send_kernel(owners, left, right, left_out, right_out, slots):
    slots_to_send(owners, slots)
    flip = axis("zl") & 1
    for i in range(16):
        right_out[i] = right[slots[2 * i + column()]]
        for core in range(2):
            for j in range(3):
                lanes = pl.ds(pl.multiple_of(lax.rem(axis("zh") + j, 4) * 128, 128), 128)
                left_out[16 * core + i, :, 128 * j : 128 * (j + 1)] = left[slots[2 * i + (core ^ flip)], :, lanes]


def theirs_kernel(acts, cots, out, some_acts, some_cots, sems):
    lanes = pl.ds(pl.multiple_of((1 - column()) * 512, 512), 512)
    copies = []
    for i in range(4):
        rows = pl.ds(256 * i, 256)
        copies.append(pltpu.make_async_copy(cots.at[rows, lanes], some_cots.at[rows], sems.at[0, i]))
        copies.append(pltpu.make_async_copy(acts.at[rows], some_acts.at[rows], sems.at[1, i]))
    for copy in copies:
        copy.start()
    acc = jnp.zeros((512, 512), F32)
    for i in range(4):
        copies[2 * i].wait()
        copies[2 * i + 1].wait()
        rows = pl.ds(256 * i, 256)
        acc += lax.dot_general(some_cots[rows, :], some_acts[rows, :], ROWS_FIRST, preferred_element_type=F32)
    out[...] = acc.astype(BF16)


def holder(owners):
    lane = lax.broadcasted_iota(jnp.int32, (1, 32), 1)
    return jnp.sum(jnp.where(lane == block_id(), owners[...], 0))


def split_kernel(mine, swapped, up, across, down, own):
    for ref, offset in ((up, 1 + 2 * column()), (across, 2), (down, 3 - 2 * column()), (own, 0)):
        first = 32 * lax.rem(axis("zl") + offset, 4)
        for h in range(4):
            rows = pl.ds(pl.multiple_of(128 * h + first, 32), 32)
            ref[32 * h : 32 * (h + 1)] = (mine[rows, :] + swapped[rows, :].astype(F32)).astype(ref.dtype)


def near_kernel(own, a, b, c, send, keep, acc):
    acc[...] = own[...] + a[...].astype(F32) + b[...].astype(F32) + c[...].astype(F32)
    other = axis("zh") + 1 + 2 * column()
    for ref, first in ((send, other), (keep, axis("zh"))):
        for j in range(2):
            rows = pl.ds(pl.multiple_of(lax.rem(first + 2 * j, 4) * 32, 32), 32)
            ref[32 * j : 32 * (j + 1)] = acc[rows, :].astype(ref.dtype)


def pair_kernel(kept, got, send, keep):
    keep[...] = kept[:32] + got[:32].astype(F32)
    send[...] = (kept[32:] + got[32:].astype(F32)).astype(BF16)


def far_kernel(owners, own, got, left, out):
    held = holder(owners)
    out[:, :512] = (own[...] + got[...].astype(F32)).astype(BF16)
    for half in range(2):
        out[16 * half : 16 * (half + 1), 512:] = left[half, held]


def middle_kernel(owners, gathered, rights, out, right, sem):
    fetch = pltpu.make_async_copy(rights.at[holder(owners)], right, sem)
    fetch.start()
    grad = gathered[:, :512]
    wide = grad.astype(F32)
    grad_sq = jnp.sum(jnp.sum(wide * wide, axis=0, keepdims=True), axis=1, keepdims=True)
    fetch.wait()
    mixed = jnp.dot(right[...], grad, preferred_element_type=F32).astype(BF16)
    mixed = mixed.T
    pieces = [mixed[128 * b : 128 * (b + 1)] for b in range(4)]
    total = jnp.zeros((128, 128), F32)
    for a in range(4):
        left = gathered[128 * a : 128 * (a + 1), 512:896]
        turn = gathered[128 * ((a + 3) % 4) : 128 * ((a + 3) % 4 + 1), 640:768]
        three = jnp.concatenate([pieces[(a + j) % 4] for j in range(3)], axis=0)
        acc = jnp.dot(left, three, preferred_element_type=F32)
        acc += lax.dot_general(turn, pieces[(a + 3) % 4], ROWS_FIRST, preferred_element_type=F32)
        total += acc * acc

        @pl.when(axis("zh") == a)
        def _():
            out[:, :16, :] = acc.astype(BF16).reshape(8, 16, 128)

    pre_sq = jnp.sum(jnp.sum(total, axis=0, keepdims=True), axis=1, keepdims=True)
    row = lax.broadcasted_iota(jnp.int32, (16, 128), 0)
    rest = jnp.where(row < 8, pre_sq, grad_sq)
    terms = jnp.zeros((16, 128), F32)
    for i in range(3):
        term = rest.astype(BF16).astype(F32)
        terms = jnp.where(row % 8 == i, term, terms)
        rest -= term
    out[:, 16:, :] = jnp.broadcast_to(terms.astype(BF16)[None], (8, 16, 128))


def place_kernel(got, out):
    def total(part, first):
        return sum(got[part, first + i : first + i + 1, :].astype(F32) for i in (2, 1, 0))

    for block in range(2):
        parts = [2 * l + (block ^ (l & 1)) for l in range(4)]
        pre_sq = sum(total(i, 16) for i in parts)
        scale = jnp.sqrt(total(parts[0], 24) / (pre_sq + 1e-06))
        for l, i in enumerate(parts):
            out[:, 512 * block + 128 * l : 512 * block + 128 * (l + 1)] = got[i, :16, :].astype(F32) * scale


def shards(activations, key_cotangent, block_owner, left_root, right_root):
    hbm = pl.BlockSpec(memory_space=pltpu.HBM)
    theirs = pl.pallas_call(
        theirs_kernel, in_specs=[hbm] * 2, out_specs=pl.BlockSpec(memory_space=pltpu.VMEM),
        out_shape=shape_of((512, 512), BF16),
        scratch_shapes=[pltpu.VMEM((1024, 512), BF16)] * 2 + [pltpu.SemaphoreType.DMA((2, 4))],
        compiler_params=pltpu.CompilerParams(vmem_limit_bytes=60 * 1024 * 1024),
    )(activations, key_cotangent)
    swapped = lax.ppermute(theirs, "core", [(0, 1), (1, 0)])
    columns = lax.dynamic_slice_in_dim(key_cotangent, column() * 512, 512, 1)
    mine = lax.dot_general(columns, activations, ROWS_FIRST, preferred_element_type=F32)

    def shift(x, step):
        moves = []
        for z in range(16):
            for block in range(2):
                to = (z + (-step if block else step)) % 16
                moves.append((2 * z + (block ^ (z & 1)), 2 * to + (block ^ (to & 1))))
        return lax.ppermute(x, ("zh", "zl", "core"), moves)

    quarter = shape_of((128, 512), BF16)
    up, across, down, own = call(
        split_kernel, (mine, swapped), (1,), [whole(512, 512)] * 2,
        [whole(128, 512)] * 4, [quarter] * 3 + [shape_of((128, 512), F32)],
    )
    a, b, c = shift(up, 1), shift(across, 2), shift(down, -1)

    owner_row = block_owner.reshape(1, 32)
    own, block_owner = lax.optimization_barrier((own, block_owner))
    left_sends, right_sends = call(
        send_kernel, (block_owner, left_root, right_root), (1,),
        [whole(4, 16, 512), pl.BlockSpec((4, 128, 512), lambda i, owners: (0, axis("zl"), 0))],
        [whole(32, 16, 384), whole(16, 128, 512)],
        [shape_of((32, 16, 384), BF16), shape_of((16, 128, 512), BF16)],
        [pltpu.SMEM((32,), jnp.int32)], prefetch=1,
    )
    own, left_sends, right_sends = lax.optimization_barrier((own, left_sends, right_sends))
    send, own = call(
        near_kernel, (own, a, b, c), (1,), [whole(128, 512)] * 4, [whole(64, 512)] * 2,
        [shape_of((64, 512), BF16), shape_of((64, 512), F32)], [pltpu.VMEM((128, 512), F32)], cost=WAIT,
    )
    own, left_sends = lax.optimization_barrier((own, left_sends))
    lefts = lax.all_to_all(left_sends, ("core", "owner"), 0, 0, tiled=True).reshape(2, 16, 16, 384)
    got = shift(send, 4)
    send, own = call(
        pair_kernel, (own, got), (1,), [whole(64, 512)] * 2, [whole(32, 512)] * 2,
        [shape_of((32, 512), BF16), shape_of((32, 512), F32)], cost=WAIT,
    )
    own, right_sends = lax.optimization_barrier((own, right_sends))
    got = shift(send, 8)
    rights = lax.all_to_all(right_sends, "owner", 0, 0, tiled=True)
    part = call(
        far_kernel, (owner_row, own, got, lefts), (1,),
        [whole(1, 32)] + [whole(32, 512)] * 2 + [whole(2, 16, 16, 384)],
        whole(32, 896), shape_of((32, 896), BF16), cost=WAIT,
    )
    groups = [[2 * z + (z & 1 ^ c) for z in range(16)] for c in range(2)]
    gathered = lax.all_gather(part, ("zh", "zl", "core"), axis=0, tiled=True, axis_index_groups=groups)

    results = call(
        middle_kernel, (owner_row, gathered, rights), (1,),
        [whole(1, 32), whole(512, 896), ANY], whole(8, 32, 128), shape_of((8, 32, 128), BF16),
        [pltpu.VMEM((128, 512), BF16), pltpu.SemaphoreType.DMA],
    )
    got = lax.all_to_all(results, ("zl", "core"), 0, 0, tiled=True)
    return call(place_kernel, (got,), (1,), [whole(8, 32, 128)], whole(16, 1024), shape_of((16, 1024), F32))


def solution(mesh):
    split = Mesh(mesh.devices.reshape(4, 4, 2, 16), ("zh", "zl", "core", "owner"))
    dp = ("zh", "zl", "core")
    in_specs = (
        P(dp, "owner"),
        P(dp, None),
        P(),
        P("owner", dp, None),
        P("owner", None, None),
    )
    out_specs = P(("owner",) + dp, None)
    return jax.shard_map(shards, mesh=split, in_specs=in_specs, out_specs=out_specs, check_vma=False)
```

```python
import jax
import jax.numpy as jnp
from jax import lax
from jax.experimental import pallas as pl
from jax.experimental.pallas import tpu as pltpu
from jax.sharding import Mesh
from jax.sharding import PartitionSpec as P

BF16 = jnp.bfloat16
F32 = jnp.float32
ROWS_FIRST = (((0,), (0,)), ((), ()))
ANY = pl.BlockSpec(memory_space=pl.ANY)


def axis(name):
    return lax.axis_index(name)


def column():
    return axis("core") ^ (axis("zl") & 1)


def block_id():
    return 2 * axis("owner") + column()


def call(kernel, args, grid, in_specs, out_specs, out_shape, scratch=(), prefetch=0, vmem=24, cost=None):
    return pl.pallas_call(
        kernel,
        grid_spec=pltpu.PrefetchScalarGridSpec(
            num_scalar_prefetch=prefetch, grid=grid, in_specs=in_specs, out_specs=out_specs, scratch_shapes=scratch
        ),
        out_shape=out_shape,
        compiler_params=pltpu.CompilerParams(vmem_limit_bytes=vmem * 1024 * 1024),
        cost_estimate=cost,
    )(*args)


WAIT = pl.CostEstimate(flops=60_000_000_000, bytes_accessed=0, transcendentals=0)


def whole(*shape):
    return pl.BlockSpec(shape, lambda i, *_: (0,) * len(shape))


def shape_of(shape, dtype):
    return jax.ShapeDtypeStruct(shape, dtype)


def slots_to_send(owners, slots):
    held = jnp.int32(0)
    for b in range(32):
        hit = owners[b] == axis("owner")
        slots[b] = jnp.where(hit, held, 0)
        held += hit.astype(jnp.int32)


def send_kernel(owners, left, right, left_out, right_out, slots):
    slots_to_send(owners, slots)
    flip = axis("zl") & 1
    for i in range(16):
        right_out[i] = right[slots[2 * i + column()]]
        for core in range(2):
            for j in range(3):
                lanes = pl.ds(pl.multiple_of(lax.rem(axis("zh") + j, 4) * 128, 128), 128)
                left_out[16 * core + i, :, 128 * j : 128 * (j + 1)] = left[slots[2 * i + (core ^ flip)], :, lanes]


def theirs_kernel(acts, cots, out, some_acts, some_cots, sems):
    lanes = pl.ds(pl.multiple_of((1 - column()) * 512, 512), 512)
    copies = []
    for i in range(4):
        rows = pl.ds(256 * i, 256)
        copies.append(pltpu.make_async_copy(cots.at[rows, lanes], some_cots.at[rows], sems.at[0, i]))
        copies.append(pltpu.make_async_copy(acts.at[rows], some_acts.at[rows], sems.at[1, i]))
    for copy in copies:
        copy.start()
    acc = jnp.zeros((512, 512), F32)
    for i in range(4):
        copies[2 * i].wait()
        copies[2 * i + 1].wait()
        rows = pl.ds(256 * i, 256)
        acc += lax.dot_general(some_cots[rows, :], some_acts[rows, :], ROWS_FIRST, preferred_element_type=F32)
    out[...] = acc.astype(BF16)


def holder(owners):
    lane = lax.broadcasted_iota(jnp.int32, (1, 32), 1)
    return jnp.sum(jnp.where(lane == block_id(), owners[...], 0))


def split_kernel(mine, swapped, up, across, down, own):
    for ref, offset in ((up, 1 + 2 * column()), (across, 2), (down, 3 - 2 * column()), (own, 0)):
        first = 32 * lax.rem(axis("zl") + offset, 4)
        for h in range(4):
            rows = pl.ds(pl.multiple_of(128 * h + first, 32), 32)
            ref[32 * h : 32 * (h + 1)] = (mine[rows, :] + swapped[rows, :].astype(F32)).astype(ref.dtype)


def near_kernel(own, a, b, c, send, keep, acc):
    acc[...] = own[...] + a[...].astype(F32) + b[...].astype(F32) + c[...].astype(F32)
    other = axis("zh") + 1 + 2 * column()
    for ref, first in ((send, other), (keep, axis("zh"))):
        for j in range(2):
            rows = pl.ds(pl.multiple_of(lax.rem(first + 2 * j, 4) * 32, 32), 32)
            ref[32 * j : 32 * (j + 1)] = acc[rows, :].astype(ref.dtype)


def pair_kernel(kept, got, send, keep):
    keep[...] = kept[:32] + got[:32].astype(F32)
    send[...] = (kept[32:] + got[32:].astype(F32)).astype(BF16)


def far_kernel(owners, own, got, left, out):
    held = holder(owners)
    out[:, :512] = (own[...] + got[...].astype(F32)).astype(BF16)
    for half in range(2):
        out[16 * half : 16 * (half + 1), 512:] = left[half, held]


def middle_kernel(owners, gathered, rights, out):
    right = rights[holder(owners)]
    grad = gathered[:, :512]
    wide = grad.astype(F32)
    grad_sq = jnp.sum(jnp.sum(wide * wide, axis=0, keepdims=True), axis=1, keepdims=True)
    mixed = jnp.dot(right, grad, preferred_element_type=F32).astype(BF16)
    mixed = mixed.T
    pieces = [mixed[128 * b : 128 * (b + 1)] for b in range(4)]
    total = jnp.zeros((128, 128), F32)
    for a in range(4):
        left = gathered[128 * a : 128 * (a + 1), 512:896]
        turn = gathered[128 * ((a + 3) % 4) : 128 * ((a + 3) % 4 + 1), 640:768]
        three = jnp.concatenate([pieces[(a + j) % 4] for j in range(3)], axis=0)
        acc = jnp.dot(left, three, preferred_element_type=F32)
        acc += lax.dot_general(turn, pieces[(a + 3) % 4], ROWS_FIRST, preferred_element_type=F32)
        total += acc * acc

        @pl.when(axis("zh") == a)
        def _():
            out[:, :16, :] = acc.astype(BF16).reshape(8, 16, 128)

    pre_sq = jnp.sum(jnp.sum(total, axis=0, keepdims=True), axis=1, keepdims=True)
    row = lax.broadcasted_iota(jnp.int32, (16, 128), 0)
    rest = jnp.where(row < 8, pre_sq, grad_sq)
    terms = jnp.zeros((16, 128), F32)
    for i in range(3):
        term = rest.astype(BF16).astype(F32)
        terms = jnp.where(row % 8 == i, term, terms)
        rest -= term
    out[:, 16:, :] = jnp.broadcast_to(terms.astype(BF16)[None], (8, 16, 128))


def place_kernel(got, out):
    def total(part, first):
        return sum(got[part, first + i : first + i + 1, :].astype(F32) for i in (2, 1, 0))

    for block in range(2):
        parts = [2 * l + (block ^ (l & 1)) for l in range(4)]
        pre_sq = sum(total(i, 16) for i in parts)
        scale = jnp.sqrt(total(parts[0], 24) / (pre_sq + 1e-06))
        for l, i in enumerate(parts):
            out[:, 512 * block + 128 * l : 512 * block + 128 * (l + 1)] = got[i, :16, :].astype(F32) * scale


def shards(activations, key_cotangent, block_owner, left_root, right_root):
    hbm = pl.BlockSpec(memory_space=pltpu.HBM)
    theirs = pl.pallas_call(
        theirs_kernel, in_specs=[hbm] * 2, out_specs=pl.BlockSpec(memory_space=pltpu.VMEM),
        out_shape=shape_of((512, 512), BF16),
        scratch_shapes=[pltpu.VMEM((1024, 512), BF16)] * 2 + [pltpu.SemaphoreType.DMA((2, 4))],
        compiler_params=pltpu.CompilerParams(vmem_limit_bytes=60 * 1024 * 1024),
    )(activations, key_cotangent)
    swapped = lax.ppermute(theirs, "core", [(0, 1), (1, 0)])
    columns = lax.dynamic_slice_in_dim(key_cotangent, column() * 512, 512, 1)
    mine = lax.dot_general(columns, activations, ROWS_FIRST, preferred_element_type=F32)

    def shift(x, step):
        moves = []
        for z in range(16):
            for block in range(2):
                to = (z + (-step if block else step)) % 16
                moves.append((2 * z + (block ^ (z & 1)), 2 * to + (block ^ (to & 1))))
        return lax.ppermute(x, ("zh", "zl", "core"), moves)

    quarter = shape_of((128, 512), BF16)
    up, across, down, own = call(
        split_kernel, (mine, swapped), (1,), [whole(512, 512)] * 2,
        [whole(128, 512)] * 4, [quarter] * 3 + [shape_of((128, 512), F32)],
    )
    a, b, c = shift(up, 1), shift(across, 2), shift(down, -1)

    owner_row = block_owner.reshape(1, 32)
    own, block_owner = lax.optimization_barrier((own, block_owner))
    left_sends, right_sends = call(
        send_kernel, (block_owner, left_root, right_root), (1,),
        [whole(4, 16, 512), pl.BlockSpec((4, 128, 512), lambda i, owners: (0, axis("zl"), 0))],
        [whole(32, 16, 384), whole(16, 128, 512)],
        [shape_of((32, 16, 384), BF16), shape_of((16, 128, 512), BF16)],
        [pltpu.SMEM((32,), jnp.int32)], prefetch=1,
    )
    own, left_sends, right_sends = lax.optimization_barrier((own, left_sends, right_sends))
    send, own = call(
        near_kernel, (own, a, b, c), (1,), [whole(128, 512)] * 4, [whole(64, 512)] * 2,
        [shape_of((64, 512), BF16), shape_of((64, 512), F32)], [pltpu.VMEM((128, 512), F32)], cost=WAIT,
    )
    own, left_sends = lax.optimization_barrier((own, left_sends))
    lefts = lax.all_to_all(left_sends, ("core", "owner"), 0, 0, tiled=True).reshape(2, 16, 16, 384)
    got = shift(send, 4)
    send, own = call(
        pair_kernel, (own, got), (1,), [whole(64, 512)] * 2, [whole(32, 512)] * 2,
        [shape_of((32, 512), BF16), shape_of((32, 512), F32)], cost=WAIT,
    )
    own, right_sends = lax.optimization_barrier((own, right_sends))
    got = shift(send, 8)
    rights = lax.all_to_all(right_sends, "owner", 0, 0, tiled=True)
    part = call(
        far_kernel, (owner_row, own, got, lefts), (1,),
        [whole(1, 32)] + [whole(32, 512)] * 2 + [whole(2, 16, 16, 384)],
        whole(32, 896), shape_of((32, 896), BF16), cost=WAIT,
    )
    groups = [[2 * z + (z & 1 ^ c) for z in range(16)] for c in range(2)]
    gathered = lax.all_gather(part, ("zh", "zl", "core"), axis=0, tiled=True, axis_index_groups=groups)

    results = call(
        middle_kernel, (owner_row, gathered, rights), (1,),
        [whole(1, 32), whole(512, 896), whole(16, 128, 512)], whole(8, 32, 128), shape_of((8, 32, 128), BF16),
    )
    got = lax.all_to_all(results, ("zl", "core"), 0, 0, tiled=True)
    return call(place_kernel, (got,), (1,), [whole(8, 32, 128)], whole(16, 1024), shape_of((16, 1024), F32))


def solution(mesh):
    split = Mesh(mesh.devices.reshape(4, 4, 2, 16), ("zh", "zl", "core", "owner"))
    dp = ("zh", "zl", "core")
    in_specs = (
        P(dp, "owner"),
        P(dp, None),
        P(),
        P("owner", dp, None),
        P("owner", None, None),
    )
    out_specs = P(("owner",) + dp, None)
    return jax.shard_map(shards, mesh=split, in_specs=in_specs, out_specs=out_specs, check_vma=False)
```

```python
import jax
import jax.numpy as jnp
from jax import lax
from jax.experimental import pallas as pl
from jax.experimental.pallas import tpu as pltpu
from jax.sharding import Mesh
from jax.sharding import PartitionSpec as P

BF16 = jnp.bfloat16
F32 = jnp.float32
ROWS_FIRST = (((0,), (0,)), ((), ()))
ANY = pl.BlockSpec(memory_space=pl.ANY)


def axis(name):
    return lax.axis_index(name)


def column():
    return axis("core") ^ (axis("zl") & 1)


def block_id():
    return 2 * axis("owner") + column()


def call(kernel, args, grid, in_specs, out_specs, out_shape, scratch=(), prefetch=0, vmem=24, cost=None):
    return pl.pallas_call(
        kernel,
        grid_spec=pltpu.PrefetchScalarGridSpec(
            num_scalar_prefetch=prefetch, grid=grid, in_specs=in_specs, out_specs=out_specs, scratch_shapes=scratch
        ),
        out_shape=out_shape,
        compiler_params=pltpu.CompilerParams(vmem_limit_bytes=vmem * 1024 * 1024),
        cost_estimate=cost,
    )(*args)


WAIT = pl.CostEstimate(flops=60_000_000_000, bytes_accessed=0, transcendentals=0)


def whole(*shape):
    return pl.BlockSpec(shape, lambda i, *_: (0,) * len(shape))


def shape_of(shape, dtype):
    return jax.ShapeDtypeStruct(shape, dtype)


def slots_to_send(owners, slots):
    held = jnp.int32(0)
    for b in range(32):
        hit = owners[b] == axis("owner")
        slots[b] = jnp.where(hit, held, 0)
        held += hit.astype(jnp.int32)


def send_kernel(owners, left, right, left_out, right_out, slots):
    slots_to_send(owners, slots)
    flip = axis("zl") & 1
    for i in range(16):
        right_out[i] = right[slots[2 * i + column()]]
        for core in range(2):
            for j in range(3):
                lanes = pl.ds(pl.multiple_of(lax.rem(axis("zh") + j, 4) * 128, 128), 128)
                left_out[16 * core + i, :, 128 * j : 128 * (j + 1)] = left[slots[2 * i + (core ^ flip)], :, lanes]


def theirs_kernel(acts, cots, out, some_acts, some_cots, staged, sems, out_sems):
    lanes = pl.ds(pl.multiple_of((1 - column()) * 512, 512), 512)
    copies = []
    for i in range(4):
        rows = pl.ds(256 * i, 256)
        copies.append(pltpu.make_async_copy(cots.at[rows, lanes], some_cots.at[rows], sems.at[0, i]))
        copies.append(pltpu.make_async_copy(acts.at[rows], some_acts.at[rows], sems.at[1, i]))
    for copy in copies:
        copy.start()
    acc = jnp.zeros((512, 512), F32)
    for i in range(3):
        copies[2 * i].wait()
        copies[2 * i + 1].wait()
        rows = pl.ds(256 * i, 256)
        acc += lax.dot_general(some_cots[rows, :], some_acts[rows, :], ROWS_FIRST, preferred_element_type=F32)
    copies[6].wait()
    copies[7].wait()
    writes = []
    for half in range(2):
        here = slice(256 * half, 256 * (half + 1))
        last = lax.dot_general(some_cots[768:, here], some_acts[768:, :], ROWS_FIRST, preferred_element_type=F32)
        staged[here] = (acc[here] + last).astype(BF16)
        rows = pl.ds(256 * half, 256)
        writes.append(pltpu.make_async_copy(staged.at[rows], out.at[rows], out_sems.at[half]))
        writes[half].start()
    for write in writes:
        write.wait()


def holder(owners):
    lane = lax.broadcasted_iota(jnp.int32, (1, 32), 1)
    return jnp.sum(jnp.where(lane == block_id(), owners[...], 0))


def split_kernel(mine, swapped, up, across, down, own):
    for ref, offset in ((up, 1 + 2 * column()), (across, 2), (down, 3 - 2 * column()), (own, 0)):
        first = 32 * lax.rem(axis("zl") + offset, 4)
        for h in range(4):
            rows = pl.ds(pl.multiple_of(128 * h + first, 32), 32)
            ref[32 * h : 32 * (h + 1)] = (mine[rows, :] + swapped[rows, :].astype(F32)).astype(ref.dtype)


def near_kernel(own, a, b, c, send, keep, acc):
    acc[...] = own[...] + a[...].astype(F32) + b[...].astype(F32) + c[...].astype(F32)
    other = axis("zh") + 1 + 2 * column()
    for ref, first in ((send, other), (keep, axis("zh"))):
        for j in range(2):
            rows = pl.ds(pl.multiple_of(lax.rem(first + 2 * j, 4) * 32, 32), 32)
            ref[32 * j : 32 * (j + 1)] = acc[rows, :].astype(ref.dtype)


def pair_kernel(kept, got, send, keep):
    keep[...] = kept[:32] + got[:32].astype(F32)
    send[...] = (kept[32:] + got[32:].astype(F32)).astype(BF16)


def far_kernel(owners, own, got, left, out):
    held = holder(owners)
    out[:, :512] = (own[...] + got[...].astype(F32)).astype(BF16)
    for half in range(2):
        out[16 * half : 16 * (half + 1), 512:] = left[half, held]


def middle_kernel(owners, gathered, rights, out):
    right = rights[holder(owners)]
    grad = gathered[:, :512]
    wide = grad.astype(F32)
    grad_sq = jnp.sum(jnp.sum(wide * wide, axis=0, keepdims=True), axis=1, keepdims=True)
    mixed = jnp.dot(right, grad, preferred_element_type=F32).astype(BF16)
    mixed = mixed.T
    pieces = [mixed[128 * b : 128 * (b + 1)] for b in range(4)]
    total = jnp.zeros((128, 128), F32)
    for a in range(4):
        left = gathered[128 * a : 128 * (a + 1), 512:896]
        turn = gathered[128 * ((a + 3) % 4) : 128 * ((a + 3) % 4 + 1), 640:768]
        three = jnp.concatenate([pieces[(a + j) % 4] for j in range(3)], axis=0)
        acc = jnp.dot(left, three, preferred_element_type=F32)
        acc += lax.dot_general(turn, pieces[(a + 3) % 4], ROWS_FIRST, preferred_element_type=F32)
        total += acc * acc

        @pl.when(axis("zh") == a)
        def _():
            out[:, :16, :] = acc.astype(BF16).reshape(8, 16, 128)

    pre_sq = jnp.sum(jnp.sum(total, axis=0, keepdims=True), axis=1, keepdims=True)
    row = lax.broadcasted_iota(jnp.int32, (16, 128), 0)
    rest = jnp.where(row < 8, pre_sq, grad_sq)
    terms = jnp.zeros((16, 128), F32)
    for i in range(3):
        term = rest.astype(BF16).astype(F32)
        terms = jnp.where(row % 8 == i, term, terms)
        rest -= term
    out[:, 16:, :] = jnp.broadcast_to(terms.astype(BF16)[None], (8, 16, 128))


def place_kernel(got, out):
    def total(part, first):
        return sum(got[part, first + i : first + i + 1, :].astype(F32) for i in (2, 1, 0))

    for block in range(2):
        parts = [2 * l + (block ^ (l & 1)) for l in range(4)]
        pre_sq = sum(total(i, 16) for i in parts)
        scale = jnp.sqrt(total(parts[0], 24) / (pre_sq + 1e-06))
        for l, i in enumerate(parts):
            out[:, 512 * block + 128 * l : 512 * block + 128 * (l + 1)] = got[i, :16, :].astype(F32) * scale


def shards(activations, key_cotangent, block_owner, left_root, right_root):
    hbm = pl.BlockSpec(memory_space=pltpu.HBM)
    theirs = pl.pallas_call(
        theirs_kernel, in_specs=[hbm] * 2, out_specs=hbm,
        out_shape=shape_of((512, 512), BF16),
        scratch_shapes=[pltpu.VMEM((1024, 512), BF16)] * 2
        + [pltpu.VMEM((512, 512), BF16), pltpu.SemaphoreType.DMA((2, 4)), pltpu.SemaphoreType.DMA((2,))],
        compiler_params=pltpu.CompilerParams(vmem_limit_bytes=60 * 1024 * 1024),
    )(activations, key_cotangent)
    swapped = lax.ppermute(theirs, "core", [(0, 1), (1, 0)])
    columns = lax.dynamic_slice_in_dim(key_cotangent, column() * 512, 512, 1)
    mine = lax.dot_general(columns, activations, ROWS_FIRST, preferred_element_type=F32)

    def shift(x, step):
        moves = []
        for z in range(16):
            for block in range(2):
                to = (z + (-step if block else step)) % 16
                moves.append((2 * z + (block ^ (z & 1)), 2 * to + (block ^ (to & 1))))
        return lax.ppermute(x, ("zh", "zl", "core"), moves)

    quarter = shape_of((128, 512), BF16)
    up, across, down, own = call(
        split_kernel, (mine, swapped), (1,), [whole(512, 512)] * 2,
        [whole(128, 512)] * 4, [quarter] * 3 + [shape_of((128, 512), F32)],
    )
    a, b, c = shift(up, 1), shift(across, 2), shift(down, -1)

    owner_row = block_owner.reshape(1, 32)
    own, block_owner = lax.optimization_barrier((own, block_owner))
    left_sends, right_sends = call(
        send_kernel, (block_owner, left_root, right_root), (1,),
        [whole(4, 16, 512), pl.BlockSpec((4, 128, 512), lambda i, owners: (0, axis("zl"), 0))],
        [whole(32, 16, 384), whole(16, 128, 512)],
        [shape_of((32, 16, 384), BF16), shape_of((16, 128, 512), BF16)],
        [pltpu.SMEM((32,), jnp.int32)], prefetch=1,
    )
    own, left_sends, right_sends = lax.optimization_barrier((own, left_sends, right_sends))
    send, own = call(
        near_kernel, (own, a, b, c), (1,), [whole(128, 512)] * 4, [whole(64, 512)] * 2,
        [shape_of((64, 512), BF16), shape_of((64, 512), F32)], [pltpu.VMEM((128, 512), F32)], cost=WAIT,
    )
    own, left_sends = lax.optimization_barrier((own, left_sends))
    lefts = lax.all_to_all(left_sends, ("core", "owner"), 0, 0, tiled=True).reshape(2, 16, 16, 384)
    got = shift(send, 4)
    send, own = call(
        pair_kernel, (own, got), (1,), [whole(64, 512)] * 2, [whole(32, 512)] * 2,
        [shape_of((32, 512), BF16), shape_of((32, 512), F32)], cost=WAIT,
    )
    own, right_sends = lax.optimization_barrier((own, right_sends))
    got = shift(send, 8)
    rights = lax.all_to_all(right_sends, "owner", 0, 0, tiled=True)
    part = call(
        far_kernel, (owner_row, own, got, lefts), (1,),
        [whole(1, 32)] + [whole(32, 512)] * 2 + [whole(2, 16, 16, 384)],
        whole(32, 896), shape_of((32, 896), BF16), cost=WAIT,
    )
    groups = [[2 * z + (z & 1 ^ c) for z in range(16)] for c in range(2)]
    gathered = lax.all_gather(part, ("zh", "zl", "core"), axis=0, tiled=True, axis_index_groups=groups)

    results = call(
        middle_kernel, (owner_row, gathered, rights), (1,),
        [whole(1, 32), whole(512, 896), whole(16, 128, 512)], whole(8, 32, 128), shape_of((8, 32, 128), BF16),
    )
    got = lax.all_to_all(results, ("zl", "core"), 0, 0, tiled=True)
    return call(place_kernel, (got,), (1,), [whole(8, 32, 128)], whole(16, 1024), shape_of((16, 1024), F32))


def solution(mesh):
    split = Mesh(mesh.devices.reshape(4, 4, 2, 16), ("zh", "zl", "core", "owner"))
    dp = ("zh", "zl", "core")
    in_specs = (
        P(dp, "owner"),
        P(dp, None),
        P(),
        P("owner", dp, None),
        P("owner", None, None),
    )
    out_specs = P(("owner",) + dp, None)
    return jax.shard_map(shards, mesh=split, in_specs=in_specs, out_specs=out_specs, check_vma=False)
```

```python
import jax
import jax.numpy as jnp
from jax import lax
from jax.experimental import pallas as pl
from jax.experimental.pallas import tpu as pltpu
from jax.sharding import Mesh
from jax.sharding import PartitionSpec as P

BF16 = jnp.bfloat16
F32 = jnp.float32
ROWS_FIRST = (((0,), (0,)), ((), ()))
ANY = pl.BlockSpec(memory_space=pl.ANY)


def axis(name):
    return lax.axis_index(name)


def column():
    return axis("core") ^ (axis("zl") & 1)


def block_id():
    return 2 * axis("owner") + column()


def call(kernel, args, grid, in_specs, out_specs, out_shape, scratch=(), prefetch=0, vmem=24, cost=None):
    return pl.pallas_call(
        kernel,
        grid_spec=pltpu.PrefetchScalarGridSpec(
            num_scalar_prefetch=prefetch, grid=grid, in_specs=in_specs, out_specs=out_specs, scratch_shapes=scratch
        ),
        out_shape=out_shape,
        compiler_params=pltpu.CompilerParams(vmem_limit_bytes=vmem * 1024 * 1024),
        cost_estimate=cost,
    )(*args)


WAIT = pl.CostEstimate(flops=60_000_000_000, bytes_accessed=0, transcendentals=0)


def whole(*shape):
    return pl.BlockSpec(shape, lambda i, *_: (0,) * len(shape))


def shape_of(shape, dtype):
    return jax.ShapeDtypeStruct(shape, dtype)


def slots_to_send(owners, slots):
    held = jnp.int32(0)
    for b in range(32):
        hit = owners[b] == axis("owner")
        slots[b] = jnp.where(hit, held, 0)
        held += hit.astype(jnp.int32)


def send_kernel(owners, left, right, left_out, right_out, slots):
    slots_to_send(owners, slots)
    flip = axis("zl") & 1
    for i in range(16):
        right_out[i] = right[slots[2 * i + column()]]
        for core in range(2):
            for j in range(3):
                lanes = pl.ds(pl.multiple_of(lax.rem(axis("zh") + j, 4) * 128, 128), 128)
                left_out[16 * core + i, :, 128 * j : 128 * (j + 1)] = left[slots[2 * i + (core ^ flip)], :, lanes]


def theirs_kernel(acts, cots, out, some_acts, some_cots, staged, sems, out_sems):
    lanes = pl.ds(pl.multiple_of((1 - column()) * 512, 512), 512)
    copies = []
    for i in range(4):
        rows = pl.ds(256 * i, 256)
        copies.append(pltpu.make_async_copy(cots.at[rows, lanes], some_cots.at[rows], sems.at[0, i]))
        copies.append(pltpu.make_async_copy(acts.at[rows], some_acts.at[rows], sems.at[1, i]))
    for copy in copies:
        copy.start()
    acc = jnp.zeros((512, 512), F32)
    for i in range(3):
        copies[2 * i].wait()
        copies[2 * i + 1].wait()
        rows = pl.ds(256 * i, 256)
        acc += lax.dot_general(some_cots[rows, :], some_acts[rows, :], ROWS_FIRST, preferred_element_type=F32)
    copies[6].wait()
    copies[7].wait()
    writes = []
    for half in range(2):
        here = slice(256 * half, 256 * (half + 1))
        last = lax.dot_general(some_cots[768:, here], some_acts[768:, :], ROWS_FIRST, preferred_element_type=F32)
        staged[here] = (acc[here] + last).astype(BF16)
        rows = pl.ds(256 * half, 256)
        writes.append(pltpu.make_async_copy(staged.at[rows], out.at[rows], out_sems.at[half]))
        writes[half].start()
    for write in writes:
        write.wait()


def holder(owners):
    lane = lax.broadcasted_iota(jnp.int32, (1, 32), 1)
    return jnp.sum(jnp.where(lane == block_id(), owners[...], 0))


def split_kernel(mine, swapped, up, across, down, own):
    for ref, offset in ((up, 1 + column()), (across, 2 + column()), (down, 3 - 2 * column()), (own, 0)):
        first = 32 * lax.rem(axis("zl") + offset, 4)
        for h in range(4):
            rows = pl.ds(pl.multiple_of(128 * h + first, 32), 32)
            ref[32 * h : 32 * (h + 1)] = (mine[rows, :] + swapped[rows, :].astype(F32)).astype(ref.dtype)


def near_kernel(own, a, b, c, send, keep, acc):
    acc[...] = own[...] + a[...].astype(F32) + b[...].astype(F32) + c[...].astype(F32)
    other = axis("zh") + 1 + 2 * column()
    for ref, first in ((send, other), (keep, axis("zh"))):
        for j in range(2):
            rows = pl.ds(pl.multiple_of(lax.rem(first + 2 * j, 4) * 32, 32), 32)
            ref[32 * j : 32 * (j + 1)] = acc[rows, :].astype(ref.dtype)


def pair_kernel(kept, got, send, keep):
    keep[...] = kept[:32] + got[:32].astype(F32)
    send[...] = (kept[32:] + got[32:].astype(F32)).astype(BF16)


def far_kernel(owners, own, got, left, out):
    held = holder(owners)
    out[:, :512] = (own[...] + got[...].astype(F32)).astype(BF16)
    for half in range(2):
        out[16 * half : 16 * (half + 1), 512:] = left[half, held]


def middle_kernel(owners, gathered, rights, out):
    right = rights[holder(owners)]
    grad = gathered[:, :512]
    wide = grad.astype(F32)
    grad_sq = jnp.sum(jnp.sum(wide * wide, axis=0, keepdims=True), axis=1, keepdims=True)
    mixed = jnp.dot(right, grad, preferred_element_type=F32).astype(BF16)
    mixed = mixed.T
    pieces = [mixed[128 * b : 128 * (b + 1)] for b in range(4)]
    total = jnp.zeros((128, 128), F32)
    for a in range(4):
        left = gathered[128 * a : 128 * (a + 1), 512:896]
        turn = gathered[128 * ((a + 3) % 4) : 128 * ((a + 3) % 4 + 1), 640:768]
        three = jnp.concatenate([pieces[(a + j) % 4] for j in range(3)], axis=0)
        acc = jnp.dot(left, three, preferred_element_type=F32)
        acc += lax.dot_general(turn, pieces[(a + 3) % 4], ROWS_FIRST, preferred_element_type=F32)
        total += acc * acc

        @pl.when(axis("zh") == a)
        def _():
            out[:, :16, :] = acc.astype(BF16).reshape(8, 16, 128)

    pre_sq = jnp.sum(jnp.sum(total, axis=0, keepdims=True), axis=1, keepdims=True)
    row = lax.broadcasted_iota(jnp.int32, (16, 128), 0)
    rest = jnp.where(row < 8, pre_sq, grad_sq)
    terms = jnp.zeros((16, 128), F32)
    for i in range(3):
        term = rest.astype(BF16).astype(F32)
        terms = jnp.where(row % 8 == i, term, terms)
        rest -= term
    out[:, 16:, :] = jnp.broadcast_to(terms.astype(BF16)[None], (8, 16, 128))


def place_kernel(got, out):
    def total(part, first):
        return sum(got[part, first + i : first + i + 1, :].astype(F32) for i in (2, 1, 0))

    for block in range(2):
        parts = [2 * l + (block ^ (l & 1)) for l in range(4)]
        pre_sq = sum(total(i, 16) for i in parts)
        scale = jnp.sqrt(total(parts[0], 24) / (pre_sq + 1e-06))
        for l, i in enumerate(parts):
            out[:, 512 * block + 128 * l : 512 * block + 128 * (l + 1)] = got[i, :16, :].astype(F32) * scale


def shards(activations, key_cotangent, block_owner, left_root, right_root):
    hbm = pl.BlockSpec(memory_space=pltpu.HBM)
    theirs = pl.pallas_call(
        theirs_kernel, in_specs=[hbm] * 2, out_specs=hbm,
        out_shape=shape_of((512, 512), BF16),
        scratch_shapes=[pltpu.VMEM((1024, 512), BF16)] * 2
        + [pltpu.VMEM((512, 512), BF16), pltpu.SemaphoreType.DMA((2, 4)), pltpu.SemaphoreType.DMA((2,))],
        compiler_params=pltpu.CompilerParams(vmem_limit_bytes=60 * 1024 * 1024),
    )(activations, key_cotangent)
    swapped = lax.ppermute(theirs, "core", [(0, 1), (1, 0)])
    columns = lax.dynamic_slice_in_dim(key_cotangent, column() * 512, 512, 1)
    mine = lax.dot_general(columns, activations, ROWS_FIRST, preferred_element_type=F32)

    def shift(x, step, other=None):
        moves = []
        for z in range(16):
            for block in range(2):
                to = (z + (-(step if other is None else other) if block else step)) % 16
                moves.append((2 * z + (block ^ (z & 1)), 2 * to + (block ^ (to & 1))))
        return lax.ppermute(x, ("zh", "zl", "core"), moves)

    quarter = shape_of((128, 512), BF16)
    up, across, down, own = call(
        split_kernel, (mine, swapped), (1,), [whole(512, 512)] * 2,
        [whole(128, 512)] * 4, [quarter] * 3 + [shape_of((128, 512), F32)],
    )
    a, b, c = shift(up, 1, 2), shift(across, 2, 1), shift(down, -1)

    owner_row = block_owner.reshape(1, 32)
    own, block_owner = lax.optimization_barrier((own, block_owner))
    left_sends, right_sends = call(
        send_kernel, (block_owner, left_root, right_root), (1,),
        [whole(4, 16, 512), pl.BlockSpec((4, 128, 512), lambda i, owners: (0, axis("zl"), 0))],
        [whole(32, 16, 384), whole(16, 128, 512)],
        [shape_of((32, 16, 384), BF16), shape_of((16, 128, 512), BF16)],
        [pltpu.SMEM((32,), jnp.int32)], prefetch=1,
    )
    own, left_sends, right_sends = lax.optimization_barrier((own, left_sends, right_sends))
    send, own = call(
        near_kernel, (own, a, b, c), (1,), [whole(128, 512)] * 4, [whole(64, 512)] * 2,
        [shape_of((64, 512), BF16), shape_of((64, 512), F32)], [pltpu.VMEM((128, 512), F32)], cost=WAIT,
    )
    own, left_sends = lax.optimization_barrier((own, left_sends))
    lefts = lax.all_to_all(left_sends, ("core", "owner"), 0, 0, tiled=True).reshape(2, 16, 16, 384)
    got = shift(send, 4)
    send, own = call(
        pair_kernel, (own, got), (1,), [whole(64, 512)] * 2, [whole(32, 512)] * 2,
        [shape_of((32, 512), BF16), shape_of((32, 512), F32)], cost=WAIT,
    )
    own, right_sends = lax.optimization_barrier((own, right_sends))
    got = shift(send, 8)
    rights = lax.all_to_all(right_sends, "owner", 0, 0, tiled=True)
    part = call(
        far_kernel, (owner_row, own, got, lefts), (1,),
        [whole(1, 32)] + [whole(32, 512)] * 2 + [whole(2, 16, 16, 384)],
        whole(32, 896), shape_of((32, 896), BF16), cost=WAIT,
    )
    groups = [[2 * z + (z & 1 ^ c) for z in range(16)] for c in range(2)]
    gathered = lax.all_gather(part, ("zh", "zl", "core"), axis=0, tiled=True, axis_index_groups=groups)

    results = call(
        middle_kernel, (owner_row, gathered, rights), (1,),
        [whole(1, 32), whole(512, 896), whole(16, 128, 512)], whole(8, 32, 128), shape_of((8, 32, 128), BF16),
    )
    got = lax.all_to_all(results, ("zl", "core"), 0, 0, tiled=True)
    return call(place_kernel, (got,), (1,), [whole(8, 32, 128)], whole(16, 1024), shape_of((16, 1024), F32))


def solution(mesh):
    split = Mesh(mesh.devices.reshape(4, 4, 2, 16), ("zh", "zl", "core", "owner"))
    dp = ("zh", "zl", "core")
    in_specs = (
        P(dp, "owner"),
        P(dp, None),
        P(),
        P("owner", dp, None),
        P("owner", None, None),
    )
    out_specs = P(("owner",) + dp, None)
    return jax.shard_map(shards, mesh=split, in_specs=in_specs, out_specs=out_specs, check_vma=False)
```

```python
import jax
import jax.numpy as jnp
from jax import lax
from jax.experimental import pallas as pl
from jax.experimental.pallas import tpu as pltpu
from jax.sharding import Mesh
from jax.sharding import PartitionSpec as P

BF16 = jnp.bfloat16
F32 = jnp.float32
ROWS_FIRST = (((0,), (0,)), ((), ()))
ANY = pl.BlockSpec(memory_space=pl.ANY)


def axis(name):
    return lax.axis_index(name)


def column():
    return axis("core") ^ (axis("zl") & 1)


def block_id():
    return 2 * axis("owner") + column()


def call(kernel, args, grid, in_specs, out_specs, out_shape, scratch=(), prefetch=0, vmem=24, cost=None):
    return pl.pallas_call(
        kernel,
        grid_spec=pltpu.PrefetchScalarGridSpec(
            num_scalar_prefetch=prefetch, grid=grid, in_specs=in_specs, out_specs=out_specs, scratch_shapes=scratch
        ),
        out_shape=out_shape,
        compiler_params=pltpu.CompilerParams(vmem_limit_bytes=vmem * 1024 * 1024),
        cost_estimate=cost,
    )(*args)


WAIT = pl.CostEstimate(flops=60_000_000_000, bytes_accessed=0, transcendentals=0)


def whole(*shape):
    return pl.BlockSpec(shape, lambda i, *_: (0,) * len(shape))


def shape_of(shape, dtype):
    return jax.ShapeDtypeStruct(shape, dtype)


def slots_to_send(owners, slots):
    held = jnp.int32(0)
    for b in range(32):
        hit = owners[b] == axis("owner")
        slots[b] = jnp.where(hit, held, 0)
        held += hit.astype(jnp.int32)


def send_kernel(owners, left, right, left_out, right_out, slots):
    slots_to_send(owners, slots)
    flip = axis("zl") & 1
    for i in range(16):
        right_out[i] = right[slots[2 * i + column()]]
        for core in range(2):
            for j in range(3):
                lanes = pl.ds(pl.multiple_of(lax.rem(axis("zh") + j, 4) * 128, 128), 128)
                left_out[16 * core + i, :, 128 * j : 128 * (j + 1)] = left[slots[2 * i + (core ^ flip)], :, lanes]


def theirs_kernel(acts, cots, out, some_acts, some_cots, staged, sems, out_sems):
    lanes = pl.ds(pl.multiple_of((1 - column()) * 512, 512), 512)
    copies = []
    for i in range(4):
        rows = pl.ds(256 * i, 256)
        copies.append(pltpu.make_async_copy(cots.at[rows, lanes], some_cots.at[rows], sems.at[0, i]))
        copies.append(pltpu.make_async_copy(acts.at[rows], some_acts.at[rows], sems.at[1, i]))
    for copy in copies:
        copy.start()
    acc = jnp.zeros((512, 512), F32)
    for i in range(3):
        copies[2 * i].wait()
        copies[2 * i + 1].wait()
        rows = pl.ds(256 * i, 256)
        acc += lax.dot_general(some_cots[rows, :], some_acts[rows, :], ROWS_FIRST, preferred_element_type=F32)
    copies[6].wait()
    copies[7].wait()
    writes = []
    for half in range(2):
        here = slice(256 * half, 256 * (half + 1))
        last = lax.dot_general(some_cots[768:, here], some_acts[768:, :], ROWS_FIRST, preferred_element_type=F32)
        staged[here] = (acc[here] + last).astype(BF16)
        rows = pl.ds(256 * half, 256)
        writes.append(pltpu.make_async_copy(staged.at[rows], out.at[rows], out_sems.at[half]))
        writes[half].start()
    for write in writes:
        write.wait()


def holder(owners):
    lane = lax.broadcasted_iota(jnp.int32, (1, 32), 1)
    return jnp.sum(jnp.where(lane == block_id(), owners[...], 0))


def split_kernel(mine, swapped, up, across, down, own):
    for ref, offset in ((up, 1 + 2 * column()), (across, 2), (down, 3 - 2 * column()), (own, 0)):
        first = 32 * lax.rem(axis("zl") + offset, 4)
        for h in range(4):
            rows = pl.ds(pl.multiple_of(128 * h + first, 32), 32)
            ref[32 * h : 32 * (h + 1)] = (mine[rows, :] + swapped[rows, :].astype(F32)).astype(ref.dtype)


def near_kernel(own, a, b, c, send, keep, acc):
    acc[...] = own[...] + a[...].astype(F32) + b[...].astype(F32) + c[...].astype(F32)
    other = axis("zh") + 1 + 2 * column()
    for ref, first in ((send, other), (keep, axis("zh"))):
        for j in range(2):
            rows = pl.ds(pl.multiple_of(lax.rem(first + 2 * j, 4) * 32, 32), 32)
            ref[32 * j : 32 * (j + 1)] = acc[rows, :].astype(ref.dtype)


def pair_kernel(kept, got, send, keep):
    keep[...] = kept[:32] + got[:32].astype(F32)
    send[...] = (kept[32:] + got[32:].astype(F32)).astype(BF16)


def far_kernel(owners, own, got, left, out):
    held = holder(owners)
    out[:, :512] = (own[...] + got[...].astype(F32)).astype(BF16)
    for half in range(2):
        out[16 * half : 16 * (half + 1), 512:] = left[half, held]


def middle_kernel(owners, gathered, rights, out):
    right = rights[holder(owners)]
    grad = gathered[:, :512]
    wide = grad.astype(F32)
    grad_sq = jnp.sum(jnp.sum(wide * wide, axis=0, keepdims=True), axis=1, keepdims=True)
    mixed = jnp.dot(right, grad, preferred_element_type=F32).astype(BF16)
    mixed = mixed.T
    pieces = [mixed[128 * b : 128 * (b + 1)] for b in range(4)]
    total = jnp.zeros((128, 128), F32)
    for a in range(4):
        left = gathered[128 * a : 128 * (a + 1), 512:896]
        turn = gathered[128 * ((a + 3) % 4) : 128 * ((a + 3) % 4 + 1), 640:768]
        three = jnp.concatenate([pieces[(a + j) % 4] for j in range(3)], axis=0)
        acc = jnp.dot(left, three, preferred_element_type=F32)
        acc += lax.dot_general(turn, pieces[(a + 3) % 4], ROWS_FIRST, preferred_element_type=F32)
        total += acc * acc

        @pl.when(axis("zh") == a)
        def _():
            out[:, :16, :] = acc.astype(BF16).reshape(8, 16, 128)

    pre_sq = jnp.sum(jnp.sum(total, axis=0, keepdims=True), axis=1, keepdims=True)
    row = lax.broadcasted_iota(jnp.int32, (16, 128), 0)
    rest = jnp.where(row < 8, pre_sq, grad_sq)
    terms = jnp.zeros((16, 128), F32)
    for i in range(3):
        term = rest.astype(BF16).astype(F32)
        terms = jnp.where(row % 8 == i, term, terms)
        rest -= term
    out[:, 16:, :] = jnp.broadcast_to(terms.astype(BF16)[None], (8, 16, 128))


def place_kernel(got, out):
    def total(part, first):
        return sum(got[part, first + i : first + i + 1, :].astype(F32) for i in (2, 1, 0))

    for block in range(2):
        parts = [2 * l + (block ^ (l & 1)) for l in range(4)]
        pre_sq = sum(total(i, 16) for i in parts)
        scale = jnp.sqrt(total(parts[0], 24) / (pre_sq + 1e-06))
        for l, i in enumerate(parts):
            out[:, 512 * block + 128 * l : 512 * block + 128 * (l + 1)] = got[i, :16, :].astype(F32) * scale


def shards(activations, key_cotangent, block_owner, left_root, right_root):
    hbm = pl.BlockSpec(memory_space=pltpu.HBM)
    theirs = pl.pallas_call(
        theirs_kernel, in_specs=[hbm] * 2, out_specs=hbm,
        out_shape=shape_of((512, 512), BF16),
        scratch_shapes=[pltpu.VMEM((1024, 512), BF16)] * 2
        + [pltpu.VMEM((512, 512), BF16), pltpu.SemaphoreType.DMA((2, 4)), pltpu.SemaphoreType.DMA((2,))],
        compiler_params=pltpu.CompilerParams(vmem_limit_bytes=60 * 1024 * 1024),
    )(activations, key_cotangent)
    swapped = lax.ppermute(theirs, "core", [(0, 1), (1, 0)])
    columns = lax.dynamic_slice_in_dim(key_cotangent, column() * 512, 512, 1)
    mine = lax.dot_general(columns, activations, ROWS_FIRST, preferred_element_type=F32)

    def shift(x, step):
        moves = []
        for z in range(16):
            for block in range(2):
                to = (z + (-step if block else step)) % 16
                moves.append((2 * z + (block ^ (z & 1)), 2 * to + (block ^ (to & 1))))
        return lax.ppermute(x, ("zh", "zl", "core"), moves)

    quarter = shape_of((128, 512), BF16)
    up, across, down, own = call(
        split_kernel, (mine, swapped), (1,), [whole(512, 512)] * 2,
        [whole(128, 512)] * 4, [quarter] * 3 + [shape_of((128, 512), F32)],
    )
    a, b, c = shift(up, 1), shift(across, -2), shift(down, -1)

    owner_row = block_owner.reshape(1, 32)
    own, block_owner = lax.optimization_barrier((own, block_owner))
    left_sends, right_sends = call(
        send_kernel, (block_owner, left_root, right_root), (1,),
        [whole(4, 16, 512), pl.BlockSpec((4, 128, 512), lambda i, owners: (0, axis("zl"), 0))],
        [whole(32, 16, 384), whole(16, 128, 512)],
        [shape_of((32, 16, 384), BF16), shape_of((16, 128, 512), BF16)],
        [pltpu.SMEM((32,), jnp.int32)], prefetch=1,
    )
    own, left_sends, right_sends = lax.optimization_barrier((own, left_sends, right_sends))
    send, own = call(
        near_kernel, (own, a, b, c), (1,), [whole(128, 512)] * 4, [whole(64, 512)] * 2,
        [shape_of((64, 512), BF16), shape_of((64, 512), F32)], [pltpu.VMEM((128, 512), F32)], cost=WAIT,
    )
    own, left_sends = lax.optimization_barrier((own, left_sends))
    lefts = lax.all_to_all(left_sends, ("core", "owner"), 0, 0, tiled=True).reshape(2, 16, 16, 384)
    got = shift(send, 4)
    send, own = call(
        pair_kernel, (own, got), (1,), [whole(64, 512)] * 2, [whole(32, 512)] * 2,
        [shape_of((32, 512), BF16), shape_of((32, 512), F32)], cost=WAIT,
    )
    own, right_sends = lax.optimization_barrier((own, right_sends))
    got = shift(send, 8)
    rights = lax.all_to_all(right_sends, "owner", 0, 0, tiled=True)
    part = call(
        far_kernel, (owner_row, own, got, lefts), (1,),
        [whole(1, 32)] + [whole(32, 512)] * 2 + [whole(2, 16, 16, 384)],
        whole(32, 896), shape_of((32, 896), BF16), cost=WAIT,
    )
    groups = [[2 * z + (z & 1 ^ c) for z in range(16)] for c in range(2)]
    gathered = lax.all_gather(part, ("zh", "zl", "core"), axis=0, tiled=True, axis_index_groups=groups)

    results = call(
        middle_kernel, (owner_row, gathered, rights), (1,),
        [whole(1, 32), whole(512, 896), whole(16, 128, 512)], whole(8, 32, 128), shape_of((8, 32, 128), BF16),
    )
    got = lax.all_to_all(results, ("zl", "core"), 0, 0, tiled=True)
    return call(place_kernel, (got,), (1,), [whole(8, 32, 128)], whole(16, 1024), shape_of((16, 1024), F32))


def solution(mesh):
    split = Mesh(mesh.devices.reshape(4, 4, 2, 16), ("zh", "zl", "core", "owner"))
    dp = ("zh", "zl", "core")
    in_specs = (
        P(dp, "owner"),
        P(dp, None),
        P(),
        P("owner", dp, None),
        P("owner", None, None),
    )
    out_specs = P(("owner",) + dp, None)
    return jax.shard_map(shards, mesh=split, in_specs=in_specs, out_specs=out_specs, check_vma=False)
```
